256 devices in a mesh: frames: 64 (over x, z, core), rows: 4 (over y).
Axes of the slice: x: 4, y: 4, z: 8, core: 2. Of those that a mesh axis runs over, the one named last changes fastest.
Arguments:
- fmap: bfloat16 [128, 12, 64, 128], P('frames', 'rows'), may hold values from -6 to 6
- context: bfloat16 [128, 12, 64, 128], P('frames', 'rows'), may hold values from -6 to 6
- pairs: int32 [256, 3], replicated, may hold values from 0 to 127, as said below
- w_corr: bfloat16 [49, 128], replicated, may hold values from -0.875 to 0.875
- w_zr: bfloat16 [256, 256], replicated, may hold values from -0.375 to 0.375
- w_q: bfloat16 [9, 256, 128], replicated, may hold values from -0.125 to 0.125
- w_msg: bfloat16 [128, 256], replicated, may hold values from -0.5 to 0.5
- w_res: bfloat16 [9, 128, 128], replicated, may hold values from -0.1875 to 0.1875
Outputs:
- state: bfloat16 [128, 12, 64, 128], P('frames', 'rows')
The draws below stay inside these ranges and needn't reach their ends.
Inputs may be any that keep to these rules, and one draw needn't show every extreme that they name: Source and target differ. With dev(f) = f // 2, the source's dev, the target's dev and the owner differ pairwise by at most one. No owner holds more than 8 pairs, and some owner holds exactly 8.
All inputs are finite; a program needn't handle non-finite values.
Results may differ from the reference program's by a relative error of at most 0.01.
Values may be sent and summed in bfloat16 or wider, within the bound.
No kernel may reach another device: no remote copies, remote signals or barrier semaphores. Data moves between devices by JAX's collectives and lax.ppermute only.
A program may use at most 64 MiB of HBM per device.

```python
import jax
import jax.numpy as jnp

CHANNELS = 128
IMG_WIDTH = 64
FRAME_DEV = 2
PAIR_DEV = 4
RADIUS = 3
ROUNDS = 2
FRAMES = 128
IMG_HEIGHT = 12
PAIR_TOTAL = 256
N_FRAMES = 64


def draw_pairs(key, part):
    keys = jax.random.split(jax.random.fold_in(key, 71), 9)
    halves = N_FRAMES // 2
    capacity = 2 * PAIR_DEV
    loads = jax.random.randint(keys[0], (halves,), 0, capacity + 1).astype(jnp.int32)
    forced = jax.random.randint(keys[1], (), 1, halves - 1).astype(jnp.int32)
    half_ids = jnp.arange(halves, dtype=jnp.int32)
    loads = jnp.where(half_ids == forced, capacity, loads).astype(jnp.int32)
    flips = jax.random.randint(keys[2], (halves,), 0, 2).astype(jnp.int32)
    evens = jnp.where(flips == 1, loads, capacity - loads).astype(jnp.int32)
    evens = jnp.where(half_ids == halves - 1, jnp.maximum(evens, 1), evens).astype(jnp.int32)
    evens = jnp.where(half_ids == 0, jnp.minimum(evens, capacity - 1), evens).astype(jnp.int32)
    counts = jnp.stack([evens, capacity - evens], axis=1).reshape(N_FRAMES).astype(jnp.int32)
    ends = jnp.cumsum(counts).astype(jnp.int32)
    positions = jnp.arange(PAIR_TOTAL, dtype=jnp.int32)
    owners = jnp.sum((positions[:, None] >= ends[None, :]).astype(jnp.int32), axis=1).astype(jnp.int32)
    src_step = jax.random.randint(keys[3], (PAIR_TOTAL,), -1, 2).astype(jnp.int32)
    src_dev = jnp.clip(owners + src_step, 0, N_FRAMES - 1).astype(jnp.int32)
    tgt_step = jax.random.randint(keys[4], (PAIR_TOTAL,), -1, 2).astype(jnp.int32)
    picker = jax.random.randint(keys[5], (PAIR_TOTAL,), 0, 2).astype(jnp.int32)
    tgt_dev = jnp.where(src_dev == owners, jnp.clip(owners + tgt_step, 0, N_FRAMES - 1), jnp.where(picker == 0, owners, src_dev)).astype(jnp.int32)
    high_first = ends[N_FRAMES - 3]
    low_first = ends[0]
    src_dev = jnp.where(positions == high_first, N_FRAMES - 2, src_dev).astype(jnp.int32)
    tgt_dev = jnp.where(positions == high_first, N_FRAMES - 1, tgt_dev).astype(jnp.int32)
    src_dev = jnp.where(positions == low_first, 0, src_dev).astype(jnp.int32)
    tgt_dev = jnp.where(positions == low_first, 1, tgt_dev).astype(jnp.int32)
    sources = (src_dev * FRAME_DEV + jax.random.randint(keys[6], (PAIR_TOTAL,), 0, FRAME_DEV)).astype(jnp.int32)
    targets = (tgt_dev * FRAME_DEV + jax.random.randint(keys[7], (PAIR_TOTAL,), 0, FRAME_DEV)).astype(jnp.int32)
    other = (src_dev * FRAME_DEV + (sources % FRAME_DEV + 1) % FRAME_DEV).astype(jnp.int32)
    targets = jnp.where(targets == sources, other, targets).astype(jnp.int32)
    table = jnp.stack([sources, targets, owners], axis=1).astype(jnp.int32)
    order = jax.random.permutation(keys[8], PAIR_TOTAL)
    return jnp.take(table, order, axis=0).astype(jnp.int32)


def shard_levels(rng, dims, shards, least, top_value):
    loudness = 1.0
    for dim, parts in shards:
        steps = jax.random.uniform(jax.random.fold_in(jax.random.fold_in(rng, 6), dim), (parts,), jnp.float32, least / len(shards), top_value / len(shards))
        loudness = loudness * jnp.repeat(jnp.exp(steps), dims[dim] // parts).reshape((-1,) + (1,) * (len(dims) - 1 - dim))
    return loudness


def bell_draw(key, extent, deviation, reach, shards=(), kind=jnp.bfloat16):
    array = jax.random.normal(key, extent, jnp.float32) * deviation
    if len(shards) > 0:
        array = shard_levels(key, extent, shards, -0.22, 0.18) * array
    return jnp.clip(array, min=-reach, max=reach).astype(kind)


def setup_inputs(seed: int = 0) -> dict:
    arg_keys = jax.random.split(jax.random.key(seed), 9)
    return {
        "fmap": bell_draw(arg_keys[0], (FRAMES, IMG_HEIGHT, IMG_WIDTH, CHANNELS), 1.0, 6.0, ((0, 64), (1, 4))),
        "context": bell_draw(arg_keys[1], (FRAMES, IMG_HEIGHT, IMG_WIDTH, CHANNELS), 1.0, 6.0, ((0, 64), (1, 4))),
        "pairs": draw_pairs(jax.random.fold_in(arg_keys[8], 71), 0),
        "w_corr": bell_draw(arg_keys[3], ((2 * RADIUS + 1) ** 2, CHANNELS), ((2 * RADIUS + 1) ** 2) ** -0.5, 0.875),
        "w_zr": bell_draw(arg_keys[4], (2 * CHANNELS, 2 * CHANNELS), (2 * CHANNELS) ** -0.5, 0.375),
        "w_q": bell_draw(arg_keys[5], (9, 2 * CHANNELS, CHANNELS), (18 * CHANNELS) ** -0.5, 0.125),
        "w_msg": bell_draw(arg_keys[6], (CHANNELS, 2 * CHANNELS), CHANNELS ** -0.5, 0.5),
        "w_res": bell_draw(arg_keys[7], (9, CHANNELS, CHANNELS), (9 * CHANNELS) ** -0.5, 0.1875),
    }


def conv_three(padded, kernel, height, width):
    count = padded.shape[0]
    cin = padded.shape[-1]
    total = None
    for row_off in range(3):
        for col_off in range(3):
            window = padded[:, row_off:row_off + height, col_off:col_off + width, :].reshape(-1, cin)
            term = jnp.dot(window, kernel[3 * row_off + col_off], preferred_element_type=jnp.float32)
            total = term if total is None else total + term
    return total.reshape(count, height, width, -1)


def pad_both(field, amount):
    return jnp.pad(field, ((0, 0), (amount, amount), (amount, amount), (0, 0)))


def reference(fmap, context, pairs, w_corr, w_zr, w_q, w_msg, w_res):
    sources = pairs[:, 0].astype(jnp.int32)
    targets = pairs[:, 1].astype(jnp.int32)
    height = fmap.shape[1]
    width = fmap.shape[2]
    chans = fmap.shape[3]
    span = 2 * RADIUS + 1
    src_feat = jnp.take(fmap, sources, axis=0).astype(jnp.float32)
    tgt_pad = pad_both(jnp.take(fmap, targets, axis=0), RADIUS)
    columns = []
    for row_off in range(span):
        for col_off in range(span):
            moved = tgt_pad[:, row_off:row_off + height, col_off:col_off + width, :].astype(jnp.float32)
            columns.append(jnp.einsum('pyxc,pyxc->pyx', src_feat, moved))
    scale = 1.0 / (chans ** 0.5)
    corr = (jnp.stack(columns, axis=-1) * scale).astype(jnp.bfloat16)
    motion = jax.nn.relu(jnp.dot(corr.reshape(-1, span * span), w_corr, preferred_element_type=jnp.float32))
    motion = motion.astype(jnp.bfloat16).reshape(-1, height, width, chans)
    state = context
    hidden = None
    for sweep in range(ROUNDS):
        ctx_src = jnp.take(state, sources, axis=0).astype(jnp.float32)
        if sweep == 0:
            hidden = jnp.tanh(ctx_src)
        xin = (motion.astype(jnp.float32) + ctx_src).astype(jnp.bfloat16)
        joined = jnp.concatenate([hidden.astype(jnp.bfloat16), xin], axis=-1)
        gates = jax.nn.sigmoid(jnp.dot(joined.reshape(-1, 2 * chans), w_zr, preferred_element_type=jnp.float32))
        gates = gates.reshape(-1, height, width, 2 * chans)
        update_gate = gates[..., :chans]
        reset_gate = gates[..., chans:]
        qin = jnp.concatenate([(reset_gate * hidden).astype(jnp.bfloat16), xin], axis=-1)
        candidate = jnp.tanh(conv_three(pad_both(qin, 1), w_q, height, width))
        hidden = (1.0 - update_gate) * hidden + update_gate * candidate
        messages = jnp.dot(hidden.astype(jnp.bfloat16).reshape(-1, chans), w_msg, preferred_element_type=jnp.float32)
        messages = messages.astype(jnp.bfloat16).reshape(-1, height, width, 2 * chans)
        incoming = jax.ops.segment_sum(messages[..., :chans].astype(jnp.float32), sources, num_segments=FRAMES)
        incoming = incoming + jax.ops.segment_sum(messages[..., chans:].astype(jnp.float32), targets, num_segments=FRAMES)
        update = jax.nn.relu(incoming).astype(jnp.bfloat16)
        state = (state.astype(jnp.float32) + conv_three(pad_both(update, 1), w_res, height, width)).astype(jnp.bfloat16)
    return state
```

```python
import jax
import jax.numpy as jnp
from jax import lax
from jax.experimental import pallas as pl
from jax.experimental.pallas import tpu as pltpu
from jax.sharding import PartitionSpec as P

SLOTS = 8
ROWS = 3
WIDTH = 64
CHANS = 128
SPAN = 7
WIDE = 5 * WIDTH
OWN = ROWS * WIDTH
F32 = jnp.float32
BF16 = jnp.bfloat16


def dot(a, b):
    return lax.dot_general(a, b, (((1,), (0,)), ((), ())), preferred_element_type=F32)


def dot_t(a, b):
    return lax.dot_general(a, b, (((1,), (1,)), ((), ())), preferred_element_type=F32)


def sigmoid(x):
    return 0.5 * jnp.tanh(0.5 * x) + 0.5


def conv_rows(field, weights, rows):
    size = rows * WIDTH
    taps = [field[k * WIDTH : k * WIDTH + size] for k in range(3)]
    out = dot(jnp.concatenate(taps, axis=1), weights)
    column = lax.broadcasted_iota(jnp.int32, (size, CHANS), 0) % WIDTH
    left = jnp.where(column == 0, 0.0, pltpu.roll(out[:, :CHANS], 1, 0))
    right = jnp.where(column == WIDTH - 1, 0.0, pltpu.roll(out[:, 2 * CHANS :], size - 1, 0))
    return out[:, CHANS : 2 * CHANS] + left + right


def gru(hidden, xin, w_zr, w_q):
    joined = jnp.concatenate([hidden.astype(BF16), xin], axis=1)
    reset = sigmoid(dot(joined, w_zr[:, CHANS:]))
    update = sigmoid(dot(joined[WIDTH : WIDTH + OWN], w_zr[:, :CHANS]))
    qin = jnp.concatenate([(reset * hidden).astype(BF16), xin], axis=1)
    candidate = jnp.tanh(conv_rows(qin, w_q, ROWS))
    own = hidden[WIDTH : WIDTH + OWN]
    return own + update * (candidate - own)


def band_mask(group):
    column = WIDTH - 1 - lax.broadcasted_iota(jnp.int32, (WIDTH, CHANS), 0)
    lane = lax.broadcasted_iota(jnp.int32, (WIDTH, CHANS), 1)
    high = lane >= WIDTH
    tap = jnp.where(high, lane - WIDTH, lane) - 8 * group - 4
    at = column + tap - 3
    keep = (tap >= 0) & (tap < SPAN) & (at >= 0) & (at < WIDTH)
    if group == 3:
        keep = keep & high
    return keep


def add_messages(acc, hidden, w_msg, source, target):
    messages = dot(hidden.astype(BF16), w_msg)
    acc[source] += messages[:, :CHANS]
    acc[target] += messages[:, CHANS:]


def first_kernel(
    idx, p0, p1, p2, p3, w_corr, w_zr, w_q, w_msg, part, hid, motion_out, feat, rim, ctx, acc
):
    pieces = (p0, p1, p2, p3)
    ends = [lax.broadcasted_iota(jnp.int32, (WIDTH, WIDTH), k) for k in range(2)]
    flip = jnp.where(ends[0] + ends[1] == WIDTH - 1, 1.0, 0.0).astype(BF16)
    acc[...] = jnp.zeros_like(acc)

    def body(s, carry):
        source, target = idx[s], idx[SLOTS + s]
        for k, piece in enumerate(pieces):

            @pl.when(source // 2 == k)
            def _():
                feat[...] = piece[source % 2, 3:8]
                ctx[...] = piece[source % 2, 11:16]

            @pl.when(target // 2 == k)
            def _():
                rim[...] = piece[target % 2, 0:11]

        rows = feat[...]
        turned = dot(flip, jnp.concatenate([rows[y] for y in range(5)], axis=1)).astype(BF16)
        corr = []
        for y in range(5):
            near = turned[:, y * CHANS : (y + 1) * CHANS]
            far = rim[y : y + SPAN].reshape(SPAN * WIDTH, CHANS)
            total = jnp.zeros((WIDTH, CHANS), F32)
            for g in range(4):
                start = 2 * WIDTH * g if g < 3 else 5 * WIDTH
                table = dot_t(near, far[start : start + 2 * WIDTH])
                moved = pltpu.roll(table, 8 * g + 72, 1, stride=1, stride_axis=0)
                total = jnp.where(band_mask(g), moved, total)
            corr.append((total * (1.0 / CHANS**0.5)).astype(BF16))
        turned = dot(flip, jnp.concatenate(corr, axis=1)).astype(BF16)
        corr = [turned[:, y * CHANS : (y + 1) * CHANS] for y in range(5)]
        motion = jnp.maximum(dot(jnp.concatenate(corr, axis=0), w_corr[...]), 0.0).astype(BF16)
        motion_out[s] = motion
        state = ctx[...].reshape(WIDE, CHANS).astype(F32)
        xin = (motion.astype(F32) + state).astype(BF16)
        hidden = gru(jnp.tanh(state), xin, w_zr[...], w_q[...])
        hid[s] = hidden
        add_messages(acc, hidden, w_msg[...], source, target)
        return carry

    lax.fori_loop(0, idx[2 * SLOTS], body, 0)
    part[...] = acc[...].astype(BF16)


def second_kernel(idx, s0, s1, motion, hid, above, below, w_zr, w_q, w_msg, part, state_buf, acc):
    acc[...] = jnp.zeros_like(acc)

    def body(s, carry):
        source, target = idx[s], idx[SLOTS + s]
        for k, piece in enumerate((s0, s1)):

            @pl.when(source // 4 == k)
            def _():
                state_buf[...] = piece[source % 4]

        state = state_buf[...].reshape(WIDE, CHANS).astype(F32)
        xin = (motion[s].astype(F32) + state).astype(BF16)
        hidden = jnp.concatenate([above[s].astype(F32), hid[s], below[s].astype(F32)], axis=0)
        hidden = gru(hidden, xin, w_zr[...], w_q[...])
        add_messages(acc, hidden, w_msg[...], source, target)
        return carry

    lax.fori_loop(0, idx[2 * SLOTS], body, 0)
    part[...] = acc[...].astype(BF16)


def state_kernel(idx, own, near, upd, above, below, w_res, out):
    row = idx[2 * SLOTS + 1]
    for frame in range(4):
        piece = own if frame < 2 else near
        field = jnp.concatenate(
            [above[frame].reshape(2 * WIDTH, CHANS), upd[frame].reshape(OWN, CHANS), below[frame].reshape(2 * WIDTH, CHANS)],
            axis=0,
        )
        base = piece[frame % 2, 11:16].reshape(WIDE, CHANS).astype(F32)
        new = (base + conv_rows(field, w_res[...], 5)).astype(BF16).reshape(5, WIDTH, CHANS)
        out[frame, 1:4] = new[1:4]
        out[frame, 0] = jnp.where(row > 0, new[0], jnp.zeros_like(new[0]))
        out[frame, 4] = jnp.where(row < 3, new[4], jnp.zeros_like(new[4]))


def last_kernel(state, upd, above, below, w_res, out):
    for frame in range(2):
        field = jnp.concatenate(
            [above[frame].reshape(WIDTH, CHANS), upd[frame].reshape(OWN, CHANS), below[frame].reshape(WIDTH, CHANS)], axis=0
        )
        base = state[frame, 1:4].reshape(OWN, CHANS).astype(F32)
        out[frame] = (base + conv_rows(field, w_res[...], ROWS)).astype(BF16).reshape(ROWS, WIDTH, CHANS)


VM = pl.BlockSpec(memory_space=pltpu.VMEM)
SM = pl.BlockSpec(memory_space=pltpu.SMEM)


def call(kernel, outs, scratch, flops, *args):
    specs = [SM if a.dtype == jnp.int32 else VM for a in args]
    size = sum(a.size * a.dtype.itemsize for a in args)
    return pl.pallas_call(
        kernel,
        out_shape=outs,
        in_specs=specs,
        out_specs=[VM] * len(outs),
        scratch_shapes=scratch,
        compiler_params=pltpu.CompilerParams(vmem_limit_bytes=24 * 2**20),
        cost_estimate=pl.CostEstimate(flops=flops, bytes_accessed=size, transcendentals=0),
    )(*args)


def slot_table(pairs, index, row):
    chip, core = index // 2, index % 2
    sources, targets, owners = (pairs[:, k] for k in range(3))

    def place(frame):
        dev = frame // 2 - 2 * chip
        other = (dev >= 1).astype(jnp.int32) != core
        beyond = (dev < 0) | (dev > 1)
        return 4 * other.astype(jnp.int32) + 2 * beyond.astype(jnp.int32) + frame % 2

    mine = (owners // 2 == chip).astype(jnp.int32)
    order = jnp.arange(pairs.shape[0], dtype=jnp.int32)
    ranks = jnp.sum(jnp.where(order[None, :] < order[:, None], mine[None, :], 0), axis=1)
    codes = place(sources) * SLOTS + place(targets)
    levels = 2 * jnp.arange(SLOTS, dtype=jnp.int32) + core
    picked = jnp.sum(jnp.where((ranks[None, :] == levels[:, None]) & (mine[None, :] == 1), codes[None, :], 0), axis=1)
    count = (jnp.sum(mine) - core + 1) // 2
    return jnp.concatenate([picked // SLOTS, picked % SLOTS, jnp.stack([count, row])])


def local(fmap, context, pairs, w_corr, w_zr, w_q, w_msg, w_res):
    index, row = lax.axis_index("frames"), lax.axis_index("rows")
    n_frames, n_rows = lax.axis_size("frames"), lax.axis_size("rows")
    up = [(i, i + 1) for i in range(n_rows - 1)]
    down = [(i + 1, i) for i in range(n_rows - 1)]
    across = [(i, (i + 2) % 4) for i in range(n_rows)]
    core_swap = [(i, i ^ 1) for i in range(n_frames)]
    chip_swap = [(i, ((i - 1) ^ 1) + 1) for i in range(1, n_frames - 1)]

    def swap_core(x):
        return lax.ppermute(x, "frames", core_swap)

    def swap_chip(x):
        return lax.ppermute(x, "frames", chip_swap)

    idx = slot_table(pairs, index, row)
    taps = w_corr.reshape(SPAN, SPAN, CHANS)
    order = (taps[0], taps[2], taps[4], jnp.zeros_like(taps[0]), taps[1], taps[3], taps[5], taps[6])
    wc = jnp.pad(jnp.stack(order), ((0, 0), (0, 1), (0, 0))).reshape(2, 32, CHANS)
    wc = jnp.pad(wc, ((0, 0), (4, 28), (0, 0))).reshape(2 * WIDTH, CHANS)
    wq = w_q.reshape(3, 3, 256, CHANS).transpose(0, 2, 1, 3).reshape(768, 384)
    wr = w_res.reshape(3, 3, CHANS, CHANS).transpose(0, 2, 1, 3).reshape(384, 384)

    with jax.named_scope("feature_rows"):
        from_above = lax.ppermute(jnp.concatenate([fmap, context[:, 2:]], axis=1), "rows", up)
        from_below = lax.ppermute(jnp.concatenate([fmap, context[:, :1]], axis=1), "rows", down)
        far = lax.ppermute(jnp.where(row < 2, fmap[:, 2:], fmap[:, :1]), "rows", across)
        none = jnp.zeros_like(far)
        own = jnp.concatenate(
            [
                jnp.where(row < 2, none, far),
                from_above[:, :3],
                fmap,
                from_below[:, :3],
                jnp.where(row < 2, far, none),
                from_above[:, 3:],
                context,
                from_below[:, 3:],
            ],
            axis=1,
        )
    with jax.named_scope("feature_window"):
        near = swap_chip(own)
        own_other = swap_core(own)
        near_other = swap_core(near)

    with jax.named_scope("first_iteration"):
        part, hid, motion = call(
            first_kernel,
            [
                jax.ShapeDtypeStruct((SLOTS, OWN, CHANS), BF16),
                jax.ShapeDtypeStruct((SLOTS, OWN, CHANS), F32),
                jax.ShapeDtypeStruct((SLOTS, WIDE, CHANS), BF16),
            ],
            [
                pltpu.VMEM((5, WIDTH, CHANS), BF16),
                pltpu.VMEM((11, WIDTH, CHANS), BF16),
                pltpu.VMEM((5, WIDTH, CHANS), BF16),
                pltpu.VMEM((SLOTS, OWN, CHANS), F32),
            ],
            2_000_000_000,
            idx, own, near, own_other, near_other, wc, w_zr, wq, w_msg,
        )

    def half_sum(part):
        return part[:4].astype(F32) + swap_core(part[4:]).astype(F32)

    with jax.named_scope("first_sums"):
        mine = half_sum(part)
        arrived = swap_chip(mine.astype(BF16)).astype(F32)
        total = mine + jnp.concatenate([arrived[2:], arrived[:2]])
        upd = jnp.maximum(total, 0.0).astype(BF16).reshape(4, ROWS, WIDTH, CHANS)
    with jax.named_scope("update_rows"):
        hid_last = hid[:, 2 * WIDTH :].astype(BF16)
        hid_first = hid[:, :WIDTH].astype(BF16)
        got_above = lax.ppermute(
            jnp.concatenate([upd[:, 1:].reshape(8, WIDTH, CHANS), hid_last]), "rows", up
        )
        got_below = lax.ppermute(
            jnp.concatenate([upd[:, :2].reshape(8, WIDTH, CHANS), hid_first]), "rows", down
        )
    with jax.named_scope("first_state"):
        [state] = call(
            state_kernel,
            [jax.ShapeDtypeStruct((4, 5, WIDTH, CHANS), BF16)],
            [],
            400_000_000,
            idx, own, near, upd, got_above[:8].reshape(4, 2, WIDTH, CHANS), got_below[:8].reshape(4, 2, WIDTH, CHANS), wr,
        )
        state_other = swap_core(state)
    with jax.named_scope("second_iteration"):
        [part] = call(
            second_kernel,
            [jax.ShapeDtypeStruct((SLOTS, OWN, CHANS), BF16)],
            [pltpu.VMEM((5, WIDTH, CHANS), BF16), pltpu.VMEM((SLOTS, OWN, CHANS), F32)],
            1_500_000_000,
            idx, state, state_other, motion, hid, got_above[8:], got_below[8:], w_zr, wq, w_msg,
        )
    with jax.named_scope("second_sums"):
        mine = half_sum(part)
        arrived = swap_chip(mine[2:].astype(BF16)).astype(F32)
        upd = jnp.maximum(mine[:2] + arrived, 0.0).astype(BF16).reshape(2, ROWS, WIDTH, CHANS)
        above = lax.ppermute(upd[:, 2:], "rows", up)
        below = lax.ppermute(upd[:, :1], "rows", down)
    with jax.named_scope("last_state"):
        [out] = call(
            last_kernel,
            [jax.ShapeDtypeStruct((2, ROWS, WIDTH, CHANS), BF16)],
            [],
            120_000_000,
            state, upd, above, below, wr,
        )
    return out


def solution(mesh):
    placed = (
        P("frames", "rows", None, None),
        P("frames", "rows", None, None),
        P(),
        P(),
        P(),
        P(),
        P(),
        P(),
    )
    return jax.shard_map(
        local,
        mesh=mesh,
        in_specs=placed,
        out_specs=P("frames", "rows", None, None),
        check_vma=False,
    )
```

```python
import jax
import jax.numpy as jnp
from jax import lax
from jax.experimental import pallas as pl
from jax.experimental.pallas import tpu as pltpu
from jax.sharding import PartitionSpec as P

SLOTS = 8
ROWS = 3
WIDTH = 64
CHANS = 128
SPAN = 7
WIDE = 5 * WIDTH
OWN = ROWS * WIDTH
F32 = jnp.float32
BF16 = jnp.bfloat16


def dot(a, b):
    return lax.dot_general(a, b, (((1,), (0,)), ((), ())), preferred_element_type=F32)


def dot_t(a, b):
    return lax.dot_general(a, b, (((1,), (1,)), ((), ())), preferred_element_type=F32)


def sigmoid(x):
    return 0.5 * jnp.tanh(0.5 * x) + 0.5


def side_by_side(weights):
    rows = [jnp.concatenate([weights[3 * k + j] for j in range(3)], axis=1) for k in range(3)]
    return jnp.concatenate(rows, axis=0)


def conv_rows(field, weights, rows):
    size = rows * WIDTH
    taps = [field[k * WIDTH : k * WIDTH + size] for k in range(3)]
    out = dot(jnp.concatenate(taps, axis=1), weights)
    column = lax.broadcasted_iota(jnp.int32, (size, CHANS), 0) % WIDTH
    left = jnp.where(column == 0, 0.0, pltpu.roll(out[:, :CHANS], 1, 0))
    right = jnp.where(column == WIDTH - 1, 0.0, pltpu.roll(out[:, 2 * CHANS :], size - 1, 0))
    return out[:, CHANS : 2 * CHANS] + left + right


def gru(hidden, xin, w_zr, w_q):
    joined = jnp.concatenate([hidden.astype(BF16), xin], axis=1)
    reset = sigmoid(dot(joined, w_zr[:, CHANS:]))
    update = sigmoid(dot(joined[WIDTH : WIDTH + OWN], w_zr[:, :CHANS]))
    qin = jnp.concatenate([(reset * hidden).astype(BF16), xin], axis=1)
    candidate = jnp.tanh(conv_rows(qin, w_q, ROWS))
    own = hidden[WIDTH : WIDTH + OWN]
    return own + update * (candidate - own)


def filled(idx):
    count = 0
    for s in range(SLOTS):
        count += jnp.where(idx[s] >= 0, 1, 0)
    return count


def band_mask(group):
    column = WIDTH - 1 - lax.broadcasted_iota(jnp.int32, (WIDTH, CHANS), 0)
    lane = lax.broadcasted_iota(jnp.int32, (WIDTH, CHANS), 1)
    high = lane >= WIDTH
    tap = jnp.where(high, lane - WIDTH, lane) - 8 * group - 4
    at = column + tap - 3
    keep = (tap >= 0) & (tap < SPAN) & (at >= 0) & (at < WIDTH)
    if group == 3:
        keep = keep & high
    return keep


def add_messages(acc, hidden, w_msg, source, target):
    messages = dot(hidden.astype(BF16), w_msg)
    acc[source] += messages[:, :CHANS]
    acc[target] += messages[:, CHANS:]


def first_kernel(
    idx, p0, p1, p2, p3, w_corr, w_zr, w_q, w_msg, part, hid, motion_out, feat, rim, ctx, acc
):
    pieces = (p0, p1, p2, p3)
    ends = [lax.broadcasted_iota(jnp.int32, (WIDTH, WIDTH), k) for k in range(2)]
    lane, tap = [lax.broadcasted_iota(jnp.int32, (CHANS, SPAN * SPAN), k) for k in range(2)]
    place = lane % WIDTH - 4
    shift = jnp.where(lane < WIDTH, 2 * (place // 8), jnp.minimum(2 * (place // 8) + 1, SPAN - 1))
    wanted = (place >= 0) & (place < 32) & (place % 8 < SPAN) & (tap == SPAN * shift + place % 8)
    spread = dot(jnp.where(wanted, 1.0, 0.0).astype(BF16), w_corr[...]).astype(BF16)
    flip = jnp.where(ends[0] + ends[1] == WIDTH - 1, 1.0, 0.0).astype(BF16)
    acc[...] = jnp.zeros_like(acc)

    def body(s, carry):
        source, target = idx[s] // SLOTS, idx[s] % SLOTS
        for k, piece in enumerate(pieces):

            @pl.when(source // 2 == k)
            def _():
                feat[...] = piece[source % 2, 3:8]
                ctx[...] = piece[source % 2, 11:16]

            @pl.when(target // 2 == k)
            def _():
                rim[...] = piece[target % 2, 0:11]

        rows = feat[...]
        turned = dot(flip, jnp.concatenate([rows[y] for y in range(5)], axis=1)).astype(BF16)
        corr = []
        for y in range(5):
            near = turned[:, y * CHANS : (y + 1) * CHANS]
            far = rim[y : y + SPAN].reshape(SPAN * WIDTH, CHANS)
            total = jnp.zeros((WIDTH, CHANS), F32)
            for g in range(4):
                start = 2 * WIDTH * g if g < 3 else 5 * WIDTH
                table = dot_t(near, far[start : start + 2 * WIDTH])
                moved = pltpu.roll(table, 8 * g + 72, 1, stride=1, stride_axis=0)
                total = jnp.where(band_mask(g), moved, total)
            corr.append((total * (1.0 / CHANS**0.5)).astype(BF16))
        turned = dot(flip, jnp.concatenate(corr, axis=1)).astype(BF16)
        corr = [turned[:, y * CHANS : (y + 1) * CHANS] for y in range(5)]
        motion = jnp.maximum(dot(jnp.concatenate(corr, axis=0), spread), 0.0).astype(BF16)
        motion_out[s] = motion
        state = ctx[...].reshape(WIDE, CHANS).astype(F32)
        xin = (motion.astype(F32) + state).astype(BF16)
        hidden = gru(jnp.tanh(state), xin, w_zr[...], side_by_side(w_q))
        hid[s] = hidden
        add_messages(acc, hidden, w_msg[...], source, target)
        return carry

    lax.fori_loop(0, filled(idx), body, 0)
    part[...] = acc[...].astype(BF16)


def second_kernel(idx, s0, s1, motion, hid, above, below, w_zr, w_q, w_msg, part, state_buf, acc):
    acc[...] = jnp.zeros_like(acc)

    def body(s, carry):
        source, target = idx[s] // SLOTS, idx[s] % SLOTS
        for k, piece in enumerate((s0, s1)):

            @pl.when(source // 4 == k)
            def _():
                state_buf[...] = piece[source % 4]

        state = state_buf[...].reshape(WIDE, CHANS).astype(F32)
        xin = (motion[s].astype(F32) + state).astype(BF16)
        row = idx[SLOTS]
        first = kept(row > 0, above[s].astype(F32))
        last = kept(row < 3, below[s].astype(F32))
        hidden = jnp.concatenate([first, hid[s], last], axis=0)
        hidden = gru(hidden, xin, w_zr[...], side_by_side(w_q))
        add_messages(acc, hidden, w_msg[...], source, target)
        return carry

    lax.fori_loop(0, filled(idx), body, 0)
    part[...] = acc[...].astype(BF16)


def kept(keep, block):
    return jnp.where(keep, block, jnp.zeros_like(block))


def state_kernel(idx, own, near, upd, above, below, w_res, out):
    row = idx[SLOTS]
    for frame in range(4):
        piece = own if frame < 2 else near
        field = jnp.concatenate(
            [
                kept(row > 0, above[frame].reshape(2 * WIDTH, CHANS)),
                upd[frame].reshape(OWN, CHANS),
                kept(row < 3, below[frame].reshape(2 * WIDTH, CHANS)),
            ],
            axis=0,
        )
        base = piece[frame % 2, 11:16].reshape(WIDE, CHANS).astype(F32)
        new = (base + conv_rows(field, side_by_side(w_res), 5)).astype(BF16).reshape(5, WIDTH, CHANS)
        out[frame, 1:4] = new[1:4]
        out[frame, 0] = kept(row > 0, new[0])
        out[frame, 4] = kept(row < 3, new[4])


def last_kernel(idx, state, upd, above, below, w_res, out):
    row = idx[SLOTS]
    for frame in range(2):
        field = jnp.concatenate(
            [
                kept(row > 0, above[frame].reshape(WIDTH, CHANS)),
                upd[frame].reshape(OWN, CHANS),
                kept(row < 3, below[frame].reshape(WIDTH, CHANS)),
            ],
            axis=0,
        )
        base = state[frame, 1:4].reshape(OWN, CHANS).astype(F32)
        out[frame] = (base + conv_rows(field, side_by_side(w_res), ROWS)).astype(BF16).reshape(ROWS, WIDTH, CHANS)


VM = pl.BlockSpec(memory_space=pltpu.VMEM)
SM = pl.BlockSpec(memory_space=pltpu.SMEM)


def call(kernel, outs, scratch, flops, *args):
    specs = [SM if a.dtype == jnp.int32 else VM for a in args]
    size = sum(a.size * a.dtype.itemsize for a in args)
    return pl.pallas_call(
        kernel,
        out_shape=outs,
        in_specs=specs,
        out_specs=[VM] * len(outs),
        scratch_shapes=scratch,
        compiler_params=pltpu.CompilerParams(vmem_limit_bytes=24 * 2**20),
        cost_estimate=pl.CostEstimate(flops=flops, bytes_accessed=size, transcendentals=0),
    )(*args)


def slot_table(pairs, index, row):
    chip, core = index >> 1, index & 1
    sources, targets, owners = (pairs[:, k] for k in range(3))

    def place(frame):
        dev = (frame >> 1) - 2 * chip
        other = jnp.where((dev >= 1) != (core == 1), 4, 0)
        return other + jnp.where((dev < 0) | (dev > 1), 2, 0) + (frame & 1)

    mine = (owners >> 1) == chip
    order = jnp.arange(pairs.shape[0], dtype=jnp.int32)
    ranks = jnp.sum(jnp.where((order[None, :] < order[:, None]) & mine[None, :], 1, 0), axis=1)
    codes = place(sources) * SLOTS + place(targets)
    levels = 2 * jnp.arange(SLOTS, dtype=jnp.int32) + core
    picked = jnp.where((ranks[None, :] == levels[:, None]) & mine[None, :], codes[None, :] + 1, 0)
    picked = jnp.sum(picked, axis=1) - 1
    return jnp.concatenate([picked, row[None]])


def local(fmap, context, pairs, w_corr, w_zr, w_q, w_msg, w_res):
    index, row = lax.axis_index("frames"), lax.axis_index("rows")
    n_frames, n_rows = lax.axis_size("frames"), lax.axis_size("rows")
    up = [(i, (i + 1) % n_rows) for i in range(n_rows)]
    down = [(j, i) for i, j in up]
    across = [(i, (i + 2) % 4) for i in range(n_rows)]
    core_swap = [(i, i ^ 1) for i in range(n_frames)]
    chip_swap = [(i, (i + 1 if i % 2 else i - 1) % n_frames) for i in range(n_frames)]

    def swap_core(x):
        return lax.ppermute(x, "frames", core_swap)

    def swap_chip(x):
        return lax.ppermute(x, "frames", chip_swap)

    with jax.named_scope("feature_rows"):
        from_above = lax.ppermute(jnp.concatenate([fmap, context[:, 2:]], axis=1), "rows", up)
        from_below = lax.ppermute(jnp.concatenate([fmap, context[:, :1]], axis=1), "rows", down)
        far = lax.ppermute(jnp.where(row < 2, fmap[:, 2:], fmap[:, :1]), "rows", across)
        none = jnp.zeros_like(far)
        from_above = jnp.where(row > 0, from_above, jnp.zeros_like(from_above))
        from_below = jnp.where(row < n_rows - 1, from_below, jnp.zeros_like(from_below))
        own = jnp.concatenate(
            [
                jnp.where(row < 2, none, far),
                from_above[:, :3],
                fmap,
                from_below[:, :3],
                jnp.where(row < 2, far, none),
                from_above[:, 3:],
                context,
                from_below[:, 3:],
            ],
            axis=1,
        )
    own, pairs = lax.optimization_barrier((own, pairs))
    idx = slot_table(pairs, index, row)
    with jax.named_scope("feature_window"):
        near = swap_chip(own)
        own_other = swap_core(own)
        near_other = swap_core(near)

    with jax.named_scope("first_iteration"):
        part, hid, motion = call(
            first_kernel,
            [
                jax.ShapeDtypeStruct((SLOTS, OWN, CHANS), BF16),
                jax.ShapeDtypeStruct((SLOTS, OWN, CHANS), F32),
                jax.ShapeDtypeStruct((SLOTS, WIDE, CHANS), BF16),
            ],
            [
                pltpu.VMEM((5, WIDTH, CHANS), BF16),
                pltpu.VMEM((11, WIDTH, CHANS), BF16),
                pltpu.VMEM((5, WIDTH, CHANS), BF16),
                pltpu.VMEM((SLOTS, OWN, CHANS), F32),
            ],
            2_000_000_000,
            idx, own, near, own_other, near_other, w_corr, w_zr, w_q, w_msg,
        )

    def half_sum(part):
        return part[:4].astype(F32) + swap_core(part[4:]).astype(F32)

    with jax.named_scope("first_sums"):
        mine = half_sum(part)
        arrived = swap_chip(mine.astype(BF16)).astype(F32)
        total = mine + jnp.concatenate([arrived[2:], arrived[:2]])
        upd = jnp.maximum(total, 0.0).astype(BF16).reshape(4, ROWS, WIDTH, CHANS)
    with jax.named_scope("update_rows"):
        hid_last = hid[:, 2 * WIDTH :].astype(BF16)
        hid_first = hid[:, :WIDTH].astype(BF16)
        got_above = lax.ppermute(
            jnp.concatenate([upd[:, 1:].reshape(8, WIDTH, CHANS), hid_last]), "rows", up
        )
        got_below = lax.ppermute(
            jnp.concatenate([upd[:, :2].reshape(8, WIDTH, CHANS), hid_first]), "rows", down
        )
    with jax.named_scope("first_state"):
        [state] = call(
            state_kernel,
            [jax.ShapeDtypeStruct((4, 5, WIDTH, CHANS), BF16)],
            [],
            400_000_000,
            idx, own, near, upd, got_above[:8].reshape(4, 2, WIDTH, CHANS), got_below[:8].reshape(4, 2, WIDTH, CHANS), w_res,
        )
        state_other = swap_core(state)
    with jax.named_scope("second_iteration"):
        [part] = call(
            second_kernel,
            [jax.ShapeDtypeStruct((SLOTS, OWN, CHANS), BF16)],
            [pltpu.VMEM((5, WIDTH, CHANS), BF16), pltpu.VMEM((SLOTS, OWN, CHANS), F32)],
            1_500_000_000,
            idx, state, state_other, motion, hid, got_above[8:], got_below[8:], w_zr, w_q, w_msg,
        )
    with jax.named_scope("second_sums"):
        mine = half_sum(part)
        arrived = swap_chip(mine[2:].astype(BF16)).astype(F32)
        upd = jnp.maximum(mine[:2] + arrived, 0.0).astype(BF16).reshape(2, ROWS, WIDTH, CHANS)
        above = lax.ppermute(upd[:, 2:], "rows", up)
        below = lax.ppermute(upd[:, :1], "rows", down)
    with jax.named_scope("last_state"):
        [out] = call(
            last_kernel,
            [jax.ShapeDtypeStruct((2, ROWS, WIDTH, CHANS), BF16)],
            [],
            120_000_000,
            idx, state, upd, above, below, w_res,
        )
    return out


def solution(mesh):
    placed = (
        P("frames", "rows", None, None),
        P("frames", "rows", None, None),
        P(),
        P(),
        P(),
        P(),
        P(),
        P(),
    )
    return jax.shard_map(
        local,
        mesh=mesh,
        in_specs=placed,
        out_specs=P("frames", "rows", None, None),
        check_vma=False,
    )
```

```python
import jax
import jax.numpy as jnp
from jax import lax
from jax.experimental import pallas as pl
from jax.experimental.pallas import tpu as pltpu
from jax.sharding import PartitionSpec as P

SLOTS = 8
ROWS = 3
WIDTH = 64
CHANS = 128
SPAN = 7
WIDE = 5 * WIDTH
OWN = ROWS * WIDTH
F32 = jnp.float32
BF16 = jnp.bfloat16


def dot(a, b):
    return lax.dot_general(a, b, (((1,), (0,)), ((), ())), preferred_element_type=F32)


def dot_t(a, b):
    return lax.dot_general(a, b, (((1,), (1,)), ((), ())), preferred_element_type=F32)


def sigmoid(x):
    return 0.5 * jnp.tanh(0.5 * x) + 0.5


def side_by_side(weights):
    rows = [jnp.concatenate([weights[3 * k + j] for j in range(3)], axis=1) for k in range(3)]
    return jnp.concatenate(rows, axis=0)


def conv_rows(fields, weights, rows):
    size = rows * WIDTH
    taps = [
        jnp.concatenate([field[k * WIDTH : k * WIDTH + size] for k in range(3)], axis=1) for field in fields
    ]
    out = dot(jnp.concatenate(taps), weights)
    size *= len(fields)
    column = lax.broadcasted_iota(jnp.int32, (size, CHANS), 0) & (WIDTH - 1)
    left = jnp.where(column == 0, 0.0, pltpu.roll(out[:, :CHANS], 1, 0))
    right = jnp.where(column == WIDTH - 1, 0.0, pltpu.roll(out[:, 2 * CHANS :], size - 1, 0))
    return out[:, CHANS : 2 * CHANS] + left + right


def gru(hidden, xin, w_zr, w_q):
    joined = [jnp.concatenate([h.astype(BF16), x], axis=1) for h, x in zip(hidden, xin)]
    own = slice(WIDTH, WIDTH + OWN)
    reset = sigmoid(dot(jnp.concatenate(joined), w_zr[:, CHANS:]))
    update = sigmoid(dot(jnp.concatenate([j[own] for j in joined]), w_zr[:, :CHANS]))
    gated = (reset * jnp.concatenate(hidden)).astype(BF16)
    fields = [jnp.concatenate([gated[k * WIDE : (k + 1) * WIDE], x], axis=1) for k, x in enumerate(xin)]
    candidate = jnp.tanh(conv_rows(fields, w_q, ROWS))
    old = jnp.concatenate([h[own] for h in hidden])
    new = old + update * (candidate - old)
    return [new[k * OWN : (k + 1) * OWN] for k in range(len(xin))]


def filled(idx):
    count = 0
    for s in range(SLOTS):
        count += jnp.where(idx[s] >= 0, 1, 0)
    return count


def add_messages(acc, idx, slots, hidden, w_msg):
    messages = dot(jnp.concatenate(hidden).astype(BF16), w_msg)
    for k, s in enumerate(slots):

        @pl.when(idx[s] >= 0)
        def _():
            acc[idx[s] // SLOTS] += messages[k * OWN : (k + 1) * OWN, :CHANS]
            acc[idx[s] % SLOTS] += messages[k * OWN : (k + 1) * OWN, CHANS:]


def give_sums(acc, part, part_other):
    part[...] = acc[:4].astype(BF16)
    part_other[...] = acc[4:].astype(BF16)


def first_kernel(
    idx, p0, p1, p2, p3, w_corr, w_zr, w_q, w_msg,
    part, part_other, hid, hid_first, hid_last, motion_out,
    feat, rim, ctx, acc, flip, spread, edge,
):
    pieces = (p0, p1, p2, p3)
    acc[...] = jnp.zeros_like(acc)
    ends = [lax.broadcasted_iota(jnp.int32, (WIDTH, WIDTH), k) for k in range(2)]
    flip[...] = jnp.where(ends[0] + ends[1] == WIDTH - 1, 1.0, 0.0).astype(BF16)
    lane, tap = [lax.broadcasted_iota(jnp.int32, (CHANS, SPAN * SPAN), k) for k in range(2)]
    place = (lane & (WIDTH - 1)) - 4
    shift = jnp.where(lane < WIDTH, 2 * (place >> 3), jnp.minimum(2 * (place >> 3) + 1, SPAN - 1))
    wanted = (place >= 0) & (place < 32) & ((place & 7) < SPAN) & (tap == SPAN * shift + (place & 7))
    spread[...] = dot(jnp.where(wanted, 1.0, 0.0).astype(BF16), w_corr[...]).astype(BF16)
    column = WIDTH - 1 - lax.broadcasted_iota(jnp.int32, (WIDTH, CHANS), 0)
    lane = lax.broadcasted_iota(jnp.int32, (WIDTH, CHANS), 1)
    place = (lane & (WIDTH - 1)) - 4
    at = column + (place & 7) - 3
    inside = (place >= 0) & (place < 32) & ((place & 7) < SPAN) & (at >= 0) & (at < WIDTH)
    inside = inside & ((place < 24) | (lane >= WIDTH))
    edge[...] = jnp.where(inside, 1.0 / CHANS**0.5, 0.0)
    place = (lax.broadcasted_iota(jnp.int32, (WIDTH, CHANS), 1) & (WIDTH - 1)) - 4

    def body(i, carry):
        slots = [2 * i + j for j in range(2)]
        for j, s in enumerate(slots):
            code = jnp.maximum(idx[s], 0)
            source, target = code // SLOTS, code % SLOTS
            for k, piece in enumerate(pieces):

                @pl.when(source // 2 == k)
                def _():
                    feat[j] = piece[source % 2, 3:8]
                    ctx[j] = piece[source % 2, 11:16]

                @pl.when(target // 2 == k)
                def _():
                    rim[j] = piece[target % 2, 0:11]

        rows = [(j, y) for j in range(2) for y in range(5)]
        turned = dot(flip[...], jnp.concatenate([feat[j, y] for j, y in rows], axis=1)).astype(BF16)
        corr = []
        for k, (j, y) in enumerate(rows):
            near = turned[:, k * CHANS : (k + 1) * CHANS]
            far = rim[j, y : y + SPAN].reshape(SPAN * WIDTH, CHANS)
            total = None
            for g in range(4):
                start = 2 * WIDTH * g if g < 3 else 5 * WIDTH
                table = dot_t(near, far[start : start + 2 * WIDTH])
                moved = pltpu.roll(table, 8 * g + 72, 1, stride=1, stride_axis=0)
                total = moved if g == 0 else jnp.where(place < 8 * g, total, moved)
            corr.append((total * edge[...]).astype(BF16))
        turned = dot(flip[...], jnp.concatenate(corr, axis=1)).astype(BF16)
        corr = jnp.concatenate([turned[:, k * CHANS : (k + 1) * CHANS] for k in range(len(rows))])
        motion = jnp.maximum(dot(corr, spread[...]), 0.0).astype(BF16)
        motion = [motion[j * WIDE : (j + 1) * WIDE] for j in range(2)]
        state = [ctx[j].reshape(WIDE, CHANS).astype(F32) for j in range(2)]
        xin = [(m.astype(F32) + c).astype(BF16) for m, c in zip(motion, state)]
        hidden = gru([jnp.tanh(c) for c in state], xin, w_zr[...], side_by_side(w_q))
        for s, m, h in zip(slots, motion, hidden):
            motion_out[s] = m
            hid[s] = h
            hid_first[s] = h[:WIDTH].astype(BF16)
            hid_last[s] = h[2 * WIDTH :].astype(BF16)
        add_messages(acc, idx, slots, hidden, w_msg[...])
        return carry

    lax.fori_loop(0, (filled(idx) + 1) // 2, body, 0)
    give_sums(acc, part, part_other)


def second_kernel(
    idx, s0, s1, motion, hid, above, below, w_zr, w_q, w_msg, part, part_other, state_buf, acc
):
    acc[...] = jnp.zeros_like(acc)
    row = idx[SLOTS]

    def body(i, carry):
        slots = [2 * i + j for j in range(2)]
        for j, s in enumerate(slots):
            source = jnp.maximum(idx[s], 0) // SLOTS
            for k, piece in enumerate((s0, s1)):

                @pl.when(source // 4 == k)
                def _():
                    state_buf[j] = piece[source % 4]

        state = [state_buf[j].reshape(WIDE, CHANS).astype(F32) for j in range(2)]
        xin = [(motion[s].astype(F32) + c).astype(BF16) for s, c in zip(slots, state)]
        hidden = [
            jnp.concatenate(
                [kept(row > 0, above[s].astype(F32)), hid[s], kept(row < 3, below[s].astype(F32))]
            )
            for s in slots
        ]
        hidden = gru(hidden, xin, w_zr[...], side_by_side(w_q))
        add_messages(acc, idx, slots, hidden, w_msg[...])
        return carry

    lax.fori_loop(0, (filled(idx) + 1) // 2, body, 0)
    give_sums(acc, part, part_other)


def kept(keep, block):
    return jnp.where(keep, block, jnp.zeros_like(block))


def state_kernel(idx, own, near, upd, above, below, w_res, out):
    row = idx[SLOTS]
    for frame in range(4):
        piece = own if frame < 2 else near
        field = jnp.concatenate(
            [
                kept(row > 0, above[frame].reshape(2 * WIDTH, CHANS)),
                upd[frame].reshape(OWN, CHANS),
                kept(row < 3, below[frame].reshape(2 * WIDTH, CHANS)),
            ],
            axis=0,
        )
        base = piece[frame % 2, 11:16].reshape(WIDE, CHANS).astype(F32)
        new = (base + conv_rows([field], side_by_side(w_res), 5)).astype(BF16).reshape(5, WIDTH, CHANS)
        out[frame, 1:4] = new[1:4]
        out[frame, 0] = kept(row > 0, new[0])
        out[frame, 4] = kept(row < 3, new[4])


def last_kernel(idx, state, upd, above, below, w_res, out):
    row = idx[SLOTS]
    for frame in range(2):
        field = jnp.concatenate(
            [
                kept(row > 0, above[frame].reshape(WIDTH, CHANS)),
                upd[frame].reshape(OWN, CHANS),
                kept(row < 3, below[frame].reshape(WIDTH, CHANS)),
            ],
            axis=0,
        )
        base = state[frame, 1:4].reshape(OWN, CHANS).astype(F32)
        out[frame] = (base + conv_rows([field], side_by_side(w_res), ROWS)).astype(BF16).reshape(ROWS, WIDTH, CHANS)


VM = pl.BlockSpec(memory_space=pltpu.VMEM)
SM = pl.BlockSpec(memory_space=pltpu.SMEM)


def call(kernel, outs, scratch, flops, *args):
    specs = [SM if a.dtype == jnp.int32 else VM for a in args]
    size = sum(a.size * a.dtype.itemsize for a in args)
    return pl.pallas_call(
        kernel,
        out_shape=outs,
        in_specs=specs,
        out_specs=[VM] * len(outs),
        scratch_shapes=scratch,
        compiler_params=pltpu.CompilerParams(vmem_limit_bytes=24 * 2**20),
        cost_estimate=pl.CostEstimate(flops=flops, bytes_accessed=size, transcendentals=0),
    )(*args)


def slot_table(pairs, index, row):
    chip, core = index >> 1, index & 1
    sources, targets, owners = (pairs[:, k] for k in range(3))

    def place(frame):
        dev = (frame >> 1) - 2 * chip
        other = jnp.where((dev >= 1) != (core == 1), 4, 0)
        return other + jnp.where((dev < 0) | (dev > 1), 2, 0) + (frame & 1)

    mine = (owners >> 1) == chip
    order = jnp.arange(pairs.shape[0], dtype=jnp.int32)
    ranks = jnp.sum(jnp.where((order[None, :] < order[:, None]) & mine[None, :], 1, 0), axis=1)
    codes = place(sources) * SLOTS + place(targets)
    levels = 2 * jnp.arange(SLOTS, dtype=jnp.int32) + core
    picked = jnp.where((ranks[None, :] == levels[:, None]) & mine[None, :], codes[None, :] + 1, 0)
    picked = jnp.sum(picked, axis=1) - 1
    return jnp.concatenate([picked, row[None]])


def local(fmap, context, pairs, w_corr, w_zr, w_q, w_msg, w_res):
    index, row = lax.axis_index("frames"), lax.axis_index("rows")
    n_frames, n_rows = lax.axis_size("frames"), lax.axis_size("rows")
    up = [(i, (i + 1) % n_rows) for i in range(n_rows)]
    down = [(j, i) for i, j in up]
    across = [(i, (i + 2) % 4) for i in range(n_rows)]
    core_swap = [(i, i ^ 1) for i in range(n_frames)]
    partner = {i: i + 1 if i % 2 else i - 1 for i in range(1, n_frames - 1)}
    chip_swap = [
        (i * n_rows + j, partner[i] * n_rows + j if i in partner else i * n_rows + (j ^ 1))
        for i in range(n_frames)
        for j in range(n_rows)
    ]

    def swap_core(x):
        return lax.ppermute(x, "frames", core_swap)

    def swap_chip(x):
        return lax.ppermute(x, ("frames", "rows"), chip_swap)

    with jax.named_scope("feature_rows"):
        from_above = lax.ppermute(jnp.concatenate([fmap, context[:, 2:]], axis=1), "rows", up)
        from_below = lax.ppermute(jnp.concatenate([fmap, context[:, :1]], axis=1), "rows", down)
        far = lax.ppermute(jnp.where(row < 2, fmap[:, 2:], fmap[:, :1]), "rows", across)
        none = jnp.zeros_like(far)
        from_above = jnp.where(row > 0, from_above, jnp.zeros_like(from_above))
        from_below = jnp.where(row < n_rows - 1, from_below, jnp.zeros_like(from_below))
        own = jnp.concatenate(
            [
                jnp.where(row < 2, none, far),
                from_above[:, :3],
                fmap,
                from_below[:, :3],
                jnp.where(row < 2, far, none),
                from_above[:, 3:],
                context,
                from_below[:, 3:],
            ],
            axis=1,
        )
    own, pairs = lax.optimization_barrier((own, pairs))
    idx = slot_table(pairs, index, row)
    with jax.named_scope("feature_window"):
        near = swap_chip(own)
        own_other = swap_core(own)
        near_other = swap_core(near)

    with jax.named_scope("first_iteration"):
        sums = [jax.ShapeDtypeStruct((4, OWN, CHANS), BF16)] * 2
        edge_rows = [jax.ShapeDtypeStruct((SLOTS, WIDTH, CHANS), BF16)] * 2
        part, part_other, hid, hid_first, hid_last, motion = call(
            first_kernel,
            [
                *sums,
                jax.ShapeDtypeStruct((SLOTS, OWN, CHANS), F32),
                *edge_rows,
                jax.ShapeDtypeStruct((SLOTS, WIDE, CHANS), BF16),
            ],
            [
                pltpu.VMEM((2, 5, WIDTH, CHANS), BF16),
                pltpu.VMEM((2, 11, WIDTH, CHANS), BF16),
                pltpu.VMEM((2, 5, WIDTH, CHANS), BF16),
                pltpu.VMEM((SLOTS, OWN, CHANS), F32),
                pltpu.VMEM((WIDTH, WIDTH), BF16),
                pltpu.VMEM((CHANS, CHANS), BF16),
                pltpu.VMEM((WIDTH, CHANS), F32),
            ],
            2_000_000_000,
            idx, own, near, own_other, near_other, w_corr, w_zr, w_q, w_msg,
        )

    with jax.named_scope("first_sums"):
        mine = part.astype(F32) + swap_core(part_other).astype(F32)
        sent = mine.astype(BF16)
        arrived = swap_chip(sent).astype(F32)
        total = mine + jnp.concatenate([arrived[2:], arrived[:2]])
        upd = jnp.maximum(total, 0.0).astype(BF16).reshape(4, ROWS, WIDTH, CHANS)
    with jax.named_scope("update_rows"):
        above = lax.ppermute(jnp.concatenate([upd[:, 1:].reshape(8, WIDTH, CHANS), hid_last]), "rows", up)
        below = lax.ppermute(jnp.concatenate([upd[:, :2].reshape(8, WIDTH, CHANS), hid_first]), "rows", down)
        upd_above, hid_above = above[:8].reshape(4, 2, WIDTH, CHANS), above[8:]
        upd_below, hid_below = below[:8].reshape(4, 2, WIDTH, CHANS), below[8:]
    with jax.named_scope("first_state"):
        [state] = call(
            state_kernel,
            [jax.ShapeDtypeStruct((4, 5, WIDTH, CHANS), BF16)],
            [],
            400_000_000,
            idx, own, near, upd, upd_above, upd_below, w_res,
        )
        state_other = swap_core(state)
    with jax.named_scope("second_iteration"):
        part, part_other = call(
            second_kernel,
            sums,
            [pltpu.VMEM((2, 5, WIDTH, CHANS), BF16), pltpu.VMEM((SLOTS, OWN, CHANS), F32)],
            1_500_000_000,
            idx, state, state_other, motion, hid, hid_above, hid_below, w_zr, w_q, w_msg,
        )
    with jax.named_scope("second_sums"):
        mine = part.astype(F32) + swap_core(part_other).astype(F32)
        arrived = swap_chip(mine[2:].astype(BF16)).astype(F32)
        upd = jnp.maximum(mine[:2] + arrived, 0.0).astype(BF16).reshape(2, ROWS, WIDTH, CHANS)
        above = lax.ppermute(upd[:, 2:], "rows", up)
        below = lax.ppermute(upd[:, :1], "rows", down)
    with jax.named_scope("last_state"):
        [out] = call(
            last_kernel,
            [jax.ShapeDtypeStruct((2, ROWS, WIDTH, CHANS), BF16)],
            [],
            120_000_000,
            idx, state, upd, above, below, w_res,
        )
    return out


def solution(mesh):
    placed = (
        P("frames", "rows", None, None),
        P("frames", "rows", None, None),
        P(),
        P(),
        P(),
        P(),
        P(),
        P(),
    )
    return jax.shard_map(
        local,
        mesh=mesh,
        in_specs=placed,
        out_specs=P("frames", "rows", None, None),
        check_vma=False,
    )
```

```python
import jax
import jax.numpy as jnp
from jax import lax
from jax.experimental import pallas as pl
from jax.experimental.pallas import tpu as pltpu
from jax.sharding import PartitionSpec as P

SLOTS = 8
ROWS = 3
WIDTH = 64
CHANS = 128
SPAN = 7
WIDE = 5 * WIDTH
OWN = ROWS * WIDTH
F32 = jnp.float32
BF16 = jnp.bfloat16


def dot(a, b):
    return lax.dot_general(a, b, (((1,), (0,)), ((), ())), preferred_element_type=F32)


def dot_t(a, b):
    return lax.dot_general(a, b, (((1,), (1,)), ((), ())), preferred_element_type=F32)


def sigmoid(x):
    return 0.5 * jnp.tanh(0.5 * x) + 0.5


def side_by_side(weights):
    rows = [jnp.concatenate([weights[3 * k + j] for j in range(3)], axis=1) for k in range(3)]
    return jnp.concatenate(rows, axis=0)


def conv_rows(fields, weights, rows):
    size = rows * WIDTH
    taps = [
        jnp.concatenate([field[k * WIDTH : k * WIDTH + size] for k in range(3)], axis=1) for field in fields
    ]
    out = dot(jnp.concatenate(taps), weights)
    size *= len(fields)
    column = lax.broadcasted_iota(jnp.int32, (size, CHANS), 0) & (WIDTH - 1)
    left = jnp.where(column == 0, 0.0, pltpu.roll(out[:, :CHANS], 1, 0))
    right = jnp.where(column == WIDTH - 1, 0.0, pltpu.roll(out[:, 2 * CHANS :], size - 1, 0))
    return out[:, CHANS : 2 * CHANS] + left + right


def gru(hidden, xin, w_zr, w_q):
    joined = [jnp.concatenate([h.astype(BF16), x], axis=1) for h, x in zip(hidden, xin)]
    own = slice(WIDTH, WIDTH + OWN)
    reset = sigmoid(dot(jnp.concatenate(joined), w_zr[:, CHANS:]))
    update = sigmoid(dot(jnp.concatenate([j[own] for j in joined]), w_zr[:, :CHANS]))
    gated = (reset * jnp.concatenate(hidden)).astype(BF16)
    fields = [jnp.concatenate([gated[k * WIDE : (k + 1) * WIDE], x], axis=1) for k, x in enumerate(xin)]
    candidate = jnp.tanh(conv_rows(fields, w_q, ROWS))
    old = jnp.concatenate([h[own] for h in hidden])
    new = old + update * (candidate - old)
    return [new[k * OWN : (k + 1) * OWN] for k in range(len(xin))]


def filled(idx):
    count = 0
    for s in range(SLOTS):
        count += jnp.where(idx[s] >= 0, 1, 0)
    return count


def add_messages(acc, idx, slots, hidden, w_msg):
    messages = dot(jnp.concatenate(hidden).astype(BF16), w_msg)
    for k, s in enumerate(slots):

        @pl.when(idx[s] >= 0)
        def _():
            acc[idx[s] // SLOTS] += messages[k * OWN : (k + 1) * OWN, :CHANS]
            acc[idx[s] % SLOTS] += messages[k * OWN : (k + 1) * OWN, CHANS:]


def give_sums(acc, part, part_other):
    part[...] = acc[:4].astype(BF16)
    part_other[...] = acc[4:].astype(BF16)


def first_kernel(
    idx, p0, p1, p2, p3, w_corr, w_zr, w_q, w_msg,
    part, part_other, hid, hid_first, hid_last, motion_out,
    feat, rim, ctx, acc, flip, spread, edge,
):
    pieces = (p0, p1, p2, p3)
    acc[...] = jnp.zeros_like(acc)
    ends = [lax.broadcasted_iota(jnp.int32, (WIDTH, WIDTH), k) for k in range(2)]
    flip[...] = jnp.where(ends[0] + ends[1] == WIDTH - 1, 1.0, 0.0).astype(BF16)
    lane, tap = [lax.broadcasted_iota(jnp.int32, (CHANS, SPAN * SPAN), k) for k in range(2)]
    place = (lane & (WIDTH - 1)) - 4
    shift = jnp.where(lane < WIDTH, 2 * (place >> 3), jnp.minimum(2 * (place >> 3) + 1, SPAN - 1))
    wanted = (place >= 0) & (place < 32) & ((place & 7) < SPAN) & (tap == SPAN * shift + (place & 7))
    spread[...] = dot(jnp.where(wanted, 1.0, 0.0).astype(BF16), w_corr[...]).astype(BF16)
    column = WIDTH - 1 - lax.broadcasted_iota(jnp.int32, (WIDTH, CHANS), 0)
    lane = lax.broadcasted_iota(jnp.int32, (WIDTH, CHANS), 1)
    place = (lane & (WIDTH - 1)) - 4
    at = column + (place & 7) - 3
    inside = (place >= 0) & (place < 32) & ((place & 7) < SPAN) & (at >= 0) & (at < WIDTH)
    inside = inside & ((place < 24) | (lane >= WIDTH))
    edge[...] = jnp.where(inside, 1.0 / CHANS**0.5, 0.0)
    place = (lax.broadcasted_iota(jnp.int32, (WIDTH, CHANS), 1) & (WIDTH - 1)) - 4

    def body(i, carry):
        slots = [2 * i + j for j in range(2)]
        for j, s in enumerate(slots):
            code = jnp.maximum(idx[s], 0)
            source, target = code // SLOTS, code % SLOTS
            for k, piece in enumerate(pieces):

                @pl.when(source // 2 == k)
                def _():
                    feat[j] = piece[source % 2, 3:8]
                    ctx[j] = piece[source % 2, 11:16]

                @pl.when(target // 2 == k)
                def _():
                    rim[j] = piece[target % 2, 0:11]

        rows = [(j, y) for j in range(2) for y in range(5)]
        turned = dot(flip[...], jnp.concatenate([feat[j, y] for j, y in rows], axis=1)).astype(BF16)
        corr = []
        for j in range(2):
            near = [turned[:, (5 * j + y) * CHANS : (5 * j + y + 1) * CHANS] for y in range(5)]
            totals = [None] * 5
            for t in range(10):
                far = rim[j, t : t + 2].reshape(2 * WIDTH, CHANS)
                uses = [(t - 2 * g, g) for g in range(3) if 0 <= t - 2 * g < 5]
                uses += [(t - 5, 3)] if t >= 5 else []
                table = dot_t(jnp.concatenate([near[y] for y, _ in uses]), far)
                for k, (y, g) in enumerate(uses):
                    part_table = table[k * WIDTH : (k + 1) * WIDTH]
                    moved = pltpu.roll(part_table, 8 * g + 72, 1, stride=1, stride_axis=0)
                    totals[y] = moved if g == 0 else jnp.where(place < 8 * g, totals[y], moved)
            corr += [(total * edge[...]).astype(BF16) for total in totals]
        turned = dot(flip[...], jnp.concatenate(corr, axis=1)).astype(BF16)
        corr = jnp.concatenate([turned[:, k * CHANS : (k + 1) * CHANS] for k in range(len(rows))])
        motion = jnp.maximum(dot(corr, spread[...]), 0.0).astype(BF16)
        motion = [motion[j * WIDE : (j + 1) * WIDE] for j in range(2)]
        state = [ctx[j].reshape(WIDE, CHANS).astype(F32) for j in range(2)]
        xin = [(m.astype(F32) + c).astype(BF16) for m, c in zip(motion, state)]
        hidden = gru([jnp.tanh(c) for c in state], xin, w_zr[...], side_by_side(w_q))
        for s, m, h in zip(slots, motion, hidden):
            motion_out[s] = m
            hid[s] = h
            hid_first[s] = h[:WIDTH].astype(BF16)
            hid_last[s] = h[2 * WIDTH :].astype(BF16)
        add_messages(acc, idx, slots, hidden, w_msg[...])
        return carry

    lax.fori_loop(0, (filled(idx) + 1) // 2, body, 0)
    give_sums(acc, part, part_other)


def second_kernel(
    idx, s0, s1, motion, hid, first, second, w_zr, w_q, w_msg, part, part_other, state_buf, acc
):
    acc[...] = jnp.zeros_like(acc)
    row = idx[SLOTS]

    def body(i, carry):
        slots = [2 * i + j for j in range(2)]
        for j, s in enumerate(slots):
            source = jnp.maximum(idx[s], 0) // SLOTS
            for k, piece in enumerate((s0, s1)):

                @pl.when(source // 4 == k)
                def _():
                    state_buf[j] = piece[source % 4]

        state = [state_buf[j].reshape(WIDE, CHANS).astype(F32) for j in range(2)]
        xin = [(motion[s].astype(F32) + c).astype(BF16) for s, c in zip(slots, state)]
        hidden = []
        for s in slots:
            above, below = arrived(row, first[SLOTS + s].astype(F32), second[SLOTS + s].astype(F32))
            hidden.append(jnp.concatenate([above, hid[s], below]))
        hidden = gru(hidden, xin, w_zr[...], side_by_side(w_q))
        add_messages(acc, idx, slots, hidden, w_msg[...])
        return carry

    lax.fori_loop(0, (filled(idx) + 1) // 2, body, 0)
    give_sums(acc, part, part_other)


def kept(keep, block):
    return jnp.where(keep, block, jnp.zeros_like(block))


def arrived(row, first, second):
    odd = row % 2 == 1
    above = kept(row > 0, jnp.where(odd, first, second))
    below = kept(row < 3, jnp.where(odd, second, first))
    return above, below


def state_kernel(idx, own, near, upd, first, second, w_res, out):
    row = idx[SLOTS]
    for half, piece in enumerate((own, near)):
        fields = []
        for frame in (2 * half, 2 * half + 1):
            rows = pl.ds(2 * frame, 2)
            above, below = arrived(row, first[rows].reshape(2 * WIDTH, CHANS), second[rows].reshape(2 * WIDTH, CHANS))
            fields.append(jnp.concatenate([above, upd[frame].reshape(OWN, CHANS), below]))
        new = conv_rows(fields, side_by_side(w_res), 5).reshape(2, 5, WIDTH, CHANS)
        new = (piece[:, 11:16].astype(F32) + new).astype(BF16)
        out[2 * half : 2 * half + 2, 1:4] = new[:, 1:4]
        out[2 * half : 2 * half + 2, 0] = kept(row > 0, new[:, 0])
        out[2 * half : 2 * half + 2, 4] = kept(row < 3, new[:, 4])


def last_kernel(idx, state, upd, first, second, w_res, out):
    row = idx[SLOTS]
    fields = []
    for frame in range(2):
        above, below = arrived(row, first[frame, 0], second[frame, 0])
        fields.append(jnp.concatenate([above, upd[frame].reshape(OWN, CHANS), below]))
    new = conv_rows(fields, side_by_side(w_res), ROWS).reshape(2, ROWS, WIDTH, CHANS)
    out[...] = (state[:2, 1:4].astype(F32) + new).astype(BF16)


VM = pl.BlockSpec(memory_space=pltpu.VMEM)
SM = pl.BlockSpec(memory_space=pltpu.SMEM)


def call(kernel, outs, scratch, flops, *args):
    specs = [SM if a.dtype == jnp.int32 else VM for a in args]
    size = sum(a.size * a.dtype.itemsize for a in args)
    return pl.pallas_call(
        kernel,
        out_shape=outs,
        in_specs=specs,
        out_specs=[VM] * len(outs),
        scratch_shapes=scratch,
        compiler_params=pltpu.CompilerParams(vmem_limit_bytes=24 * 2**20),
        cost_estimate=pl.CostEstimate(flops=flops, bytes_accessed=size, transcendentals=0),
    )(*args)


def slot_table(pairs, index, row):
    chip, core = index >> 1, index & 1
    sources, targets, owners = (pairs[:, k] for k in range(3))

    def place(frame):
        dev = (frame >> 1) - 2 * chip
        other = jnp.where((dev >= 1) != (core == 1), 4, 0)
        return other + jnp.where((dev < 0) | (dev > 1), 2, 0) + (frame & 1)

    mine = (owners >> 1) == chip
    order = jnp.arange(pairs.shape[0], dtype=jnp.int32)
    ranks = jnp.sum(jnp.where((order[None, :] < order[:, None]) & mine[None, :], 1, 0), axis=1)
    codes = place(sources) * SLOTS + place(targets)
    levels = 2 * jnp.arange(SLOTS, dtype=jnp.int32) + core
    picked = jnp.where((ranks[None, :] == levels[:, None]) & mine[None, :], codes[None, :] + 1, 0)
    picked = jnp.sum(picked, axis=1) - 1
    return jnp.concatenate([picked, row[None]])


def local(fmap, context, pairs, w_corr, w_zr, w_q, w_msg, w_res):
    index, row = lax.axis_index("frames"), lax.axis_index("rows")
    n_frames, n_rows = lax.axis_size("frames"), lax.axis_size("rows")
    even_swap = [(i, i ^ 1) for i in range(n_rows)]
    odd_swap = [(i, n_rows - 1 - i) for i in range(n_rows)]
    odd = row % 2 == 1
    across = [(i, (i + 2) % 4) for i in range(n_rows)]
    core_swap = [(i, i ^ 1) for i in range(n_frames)]
    partner = {i: i + 1 if i % 2 else i - 1 for i in range(1, n_frames - 1)}
    chip_swap = [
        (i * n_rows + j, partner[i] * n_rows + j if i in partner else i * n_rows + (j ^ 1))
        for i in range(n_frames)
        for j in range(n_rows)
    ]

    def rows_swaps(to_above, to_below):
        first = lax.ppermute(jnp.where(odd, to_above, to_below), "rows", even_swap)
        second = lax.ppermute(jnp.where(odd, to_below, to_above), "rows", odd_swap)
        return first, second

    def swap_core(x):
        return lax.ppermute(x, "frames", core_swap)

    def swap_chip(x):
        return lax.ppermute(x, ("frames", "rows"), chip_swap)

    with jax.named_scope("feature_rows"):
        far = lax.ppermute(jnp.where(row < 2, fmap[:, 2:], fmap[:, :1]), "rows", across)
        first, second = rows_swaps(
            jnp.concatenate([fmap, context[:, :1]], axis=1), jnp.concatenate([fmap, context[:, 2:]], axis=1)
        )
        none = jnp.zeros_like(far)
        blank = jnp.zeros_like(first)
        from_above = jnp.where(row > 0, jnp.where(odd, first, second), blank)
        from_below = jnp.where(row < n_rows - 1, jnp.where(odd, second, first), blank)
        own = jnp.concatenate(
            [
                jnp.where(row < 2, none, far),
                from_above[:, :3],
                fmap,
                from_below[:, :3],
                jnp.where(row < 2, far, none),
                from_above[:, 3:],
                context,
                from_below[:, 3:],
            ],
            axis=1,
        )
    own, pairs = lax.optimization_barrier((own, pairs))
    idx = slot_table(pairs, index, row)
    with jax.named_scope("feature_window"):
        near = swap_chip(own)
        own_other = swap_core(own)
        near_other = swap_core(near)

    with jax.named_scope("first_iteration"):
        sums = [jax.ShapeDtypeStruct((4, OWN, CHANS), BF16)] * 2
        edge_rows = [jax.ShapeDtypeStruct((SLOTS, WIDTH, CHANS), BF16)] * 2
        part, part_other, hid, hid_first, hid_last, motion = call(
            first_kernel,
            [
                *sums,
                jax.ShapeDtypeStruct((SLOTS, OWN, CHANS), F32),
                *edge_rows,
                jax.ShapeDtypeStruct((SLOTS, WIDE, CHANS), BF16),
            ],
            [
                pltpu.VMEM((2, 5, WIDTH, CHANS), BF16),
                pltpu.VMEM((2, 11, WIDTH, CHANS), BF16),
                pltpu.VMEM((2, 5, WIDTH, CHANS), BF16),
                pltpu.VMEM((SLOTS, OWN, CHANS), F32),
                pltpu.VMEM((WIDTH, WIDTH), BF16),
                pltpu.VMEM((CHANS, CHANS), BF16),
                pltpu.VMEM((WIDTH, CHANS), F32),
            ],
            2_000_000_000,
            idx, own, near, own_other, near_other, w_corr, w_zr, w_q, w_msg,
        )

    with jax.named_scope("first_sums"):
        mine = part.astype(F32) + swap_core(part_other).astype(F32)
        sent = mine.astype(BF16)
        arrived = swap_chip(sent).astype(F32)
        total = mine + jnp.concatenate([arrived[2:], arrived[:2]])
        upd = jnp.maximum(total, 0.0).astype(BF16).reshape(4, ROWS, WIDTH, CHANS)
    with jax.named_scope("update_rows"):
        first, second = rows_swaps(
            jnp.concatenate([upd[:, :2].reshape(8, WIDTH, CHANS), hid_first]),
            jnp.concatenate([upd[:, 1:].reshape(8, WIDTH, CHANS), hid_last]),
        )
    with jax.named_scope("first_state"):
        [state] = call(
            state_kernel,
            [jax.ShapeDtypeStruct((4, 5, WIDTH, CHANS), BF16)],
            [],
            400_000_000,
            idx, own, near, upd, first, second, w_res,
        )
        state_other = swap_core(state)
    with jax.named_scope("second_iteration"):
        part, part_other = call(
            second_kernel,
            sums,
            [pltpu.VMEM((2, 5, WIDTH, CHANS), BF16), pltpu.VMEM((SLOTS, OWN, CHANS), F32)],
            1_500_000_000,
            idx, state, state_other, motion, hid, first, second, w_zr, w_q, w_msg,
        )
    with jax.named_scope("second_sums"):
        mine = part.astype(F32) + swap_core(part_other).astype(F32)
        arrived = swap_chip(mine[2:].astype(BF16)).astype(F32)
        upd = jnp.maximum(mine[:2] + arrived, 0.0).astype(BF16).reshape(2, ROWS, WIDTH, CHANS)
        first, second = rows_swaps(upd[:, :1], upd[:, 2:])
    with jax.named_scope("last_state"):
        [out] = call(
            last_kernel,
            [jax.ShapeDtypeStruct((2, ROWS, WIDTH, CHANS), BF16)],
            [],
            120_000_000,
            idx, state, upd, first, second, w_res,
        )
    return out


def solution(mesh):
    placed = (
        P("frames", "rows", None, None),
        P("frames", "rows", None, None),
        P(),
        P(),
        P(),
        P(),
        P(),
        P(),
    )
    return jax.shard_map(
        local,
        mesh=mesh,
        in_specs=placed,
        out_specs=P("frames", "rows", None, None),
        check_vma=False,
    )
```

```python
import jax
import jax.numpy as jnp
from jax import lax
from jax.experimental import pallas as pl
from jax.experimental.pallas import tpu as pltpu
from jax.sharding import PartitionSpec as P

SLOTS = 8
ROWS = 3
WIDTH = 64
CHANS = 128
SPAN = 7
WIDE = 5 * WIDTH
OWN = ROWS * WIDTH
F32 = jnp.float32
BF16 = jnp.bfloat16


def dot(a, b):
    return lax.dot_general(a, b, (((1,), (0,)), ((), ())), preferred_element_type=F32)


def dot_t(a, b):
    return lax.dot_general(a, b, (((1,), (1,)), ((), ())), preferred_element_type=F32)


def sigmoid(x):
    return 0.5 * jnp.tanh(0.5 * x) + 0.5


def side_by_side(weights):
    rows = [jnp.concatenate([weights[3 * k + j] for j in range(3)], axis=1) for k in range(3)]
    return jnp.concatenate(rows, axis=0)


def conv_rows(fields, weights, rows):
    size = rows * WIDTH
    taps = [
        jnp.concatenate([field[k * WIDTH : k * WIDTH + size] for k in range(3)], axis=1) for field in fields
    ]
    out = dot(jnp.concatenate(taps), weights)
    size *= len(fields)
    column = lax.broadcasted_iota(jnp.int32, (size, CHANS), 0) & (WIDTH - 1)
    left = jnp.where(column == 0, 0.0, pltpu.roll(out[:, :CHANS], 1, 0))
    right = jnp.where(column == WIDTH - 1, 0.0, pltpu.roll(out[:, 2 * CHANS :], size - 1, 0))
    return out[:, CHANS : 2 * CHANS] + left + right


def gru(hidden, xin, w_zr, w_q):
    joined = [jnp.concatenate([h.astype(BF16), x], axis=1) for h, x in zip(hidden, xin)]
    own = slice(WIDTH, WIDTH + OWN)
    reset = sigmoid(dot(jnp.concatenate(joined), w_zr[:, CHANS:]))
    update = sigmoid(dot(jnp.concatenate([j[own] for j in joined]), w_zr[:, :CHANS]))
    gated = (reset * jnp.concatenate(hidden)).astype(BF16)
    fields = [jnp.concatenate([gated[k * WIDE : (k + 1) * WIDE], x], axis=1) for k, x in enumerate(xin)]
    candidate = jnp.tanh(conv_rows(fields, w_q, ROWS))
    old = jnp.concatenate([h[own] for h in hidden])
    new = old + update * (candidate - old)
    return [new[k * OWN : (k + 1) * OWN] for k in range(len(xin))]


def read_table(table, idx):
    count = 0
    for s in range(SLOTS):
        code = table[0, s]
        idx[s] = code
        count += jnp.where(code >= 0, 1, 0)
    return count


def add_messages(acc, idx, slots, hidden, w_msg):
    messages = dot(jnp.concatenate(hidden).astype(BF16), w_msg)
    for k, s in enumerate(slots):

        @pl.when(idx[s] >= 0)
        def _():
            acc[idx[s] // SLOTS] += messages[k * OWN : (k + 1) * OWN, :CHANS]
            acc[idx[s] % SLOTS] += messages[k * OWN : (k + 1) * OWN, CHANS:]


def give_sums(acc, part, part_other):
    part[...] = acc[:4].astype(BF16)
    part_other[...] = acc[4:].astype(BF16)


def first_kernel(
    table, p0, p1, p2, p3, w_corr, w_zr, w_q, w_msg,
    part, part_other, hid, hid_first, hid_last, motion_out,
    feat, rim, ctx, acc, flip, spread, edge, idx,
):
    pieces = (p0, p1, p2, p3)
    count = read_table(table, idx)
    acc[...] = jnp.zeros_like(acc)
    ends = [lax.broadcasted_iota(jnp.int32, (WIDTH, WIDTH), k) for k in range(2)]
    flip[...] = jnp.where(ends[0] + ends[1] == WIDTH - 1, 1.0, 0.0).astype(BF16)
    lane, tap = [lax.broadcasted_iota(jnp.int32, (CHANS, SPAN * SPAN), k) for k in range(2)]
    place = (lane & (WIDTH - 1)) - 4
    shift = jnp.where(lane < WIDTH, 2 * (place >> 3), jnp.minimum(2 * (place >> 3) + 1, SPAN - 1))
    wanted = (place >= 0) & (place < 32) & ((place & 7) < SPAN) & (tap == SPAN * shift + (place & 7))
    spread[...] = dot(jnp.where(wanted, 1.0, 0.0).astype(BF16), w_corr[...]).astype(BF16)
    column = WIDTH - 1 - lax.broadcasted_iota(jnp.int32, (WIDTH, CHANS), 0)
    lane = lax.broadcasted_iota(jnp.int32, (WIDTH, CHANS), 1)
    place = (lane & (WIDTH - 1)) - 4
    at = column + (place & 7) - 3
    inside = (place >= 0) & (place < 32) & ((place & 7) < SPAN) & (at >= 0) & (at < WIDTH)
    inside = inside & ((place < 24) | (lane >= WIDTH))
    edge[...] = jnp.where(inside, 1.0 / CHANS**0.5, 0.0)
    place = (lax.broadcasted_iota(jnp.int32, (WIDTH, CHANS), 1) & (WIDTH - 1)) - 4

    def body(i, carry):
        slots = [2 * i + j for j in range(2)]
        for j, s in enumerate(slots):
            code = jnp.maximum(idx[s], 0)
            source, target = code // SLOTS, code % SLOTS
            for k, piece in enumerate(pieces):

                @pl.when(source // 2 == k)
                def _():
                    feat[j] = piece[source % 2, 3:8]
                    ctx[j] = piece[source % 2, 11:16]

                @pl.when(target // 2 == k)
                def _():
                    rim[j] = piece[target % 2, 0:11]

        rows = [(j, y) for j in range(2) for y in range(5)]
        turned = dot(flip[...], jnp.concatenate([feat[j, y] for j, y in rows], axis=1)).astype(BF16)
        corr = []
        for j in range(2):
            near = [turned[:, (5 * j + y) * CHANS : (5 * j + y + 1) * CHANS] for y in range(5)]
            totals = [None] * 5
            for t in range(10):
                far = rim[j, t : t + 2].reshape(2 * WIDTH, CHANS)
                uses = [(t - 2 * g, g) for g in range(3) if 0 <= t - 2 * g < 5]
                uses += [(t - 5, 3)] if t >= 5 else []
                table = dot_t(jnp.concatenate([near[y] for y, _ in uses]), far)
                for k, (y, g) in enumerate(uses):
                    part_table = table[k * WIDTH : (k + 1) * WIDTH]
                    moved = pltpu.roll(part_table, 8 * g + 72, 1, stride=1, stride_axis=0)
                    totals[y] = moved if g == 0 else jnp.where(place < 8 * g, totals[y], moved)
            corr += [(total * edge[...]).astype(BF16) for total in totals]
        turned = dot(flip[...], jnp.concatenate(corr, axis=1)).astype(BF16)
        corr = jnp.concatenate([turned[:, k * CHANS : (k + 1) * CHANS] for k in range(len(rows))])
        motion = jnp.maximum(dot(corr, spread[...]), 0.0).astype(BF16)
        motion = [motion[j * WIDE : (j + 1) * WIDE] for j in range(2)]
        state = [ctx[j].reshape(WIDE, CHANS).astype(F32) for j in range(2)]
        xin = [(m.astype(F32) + c).astype(BF16) for m, c in zip(motion, state)]
        hidden = gru([jnp.tanh(c) for c in state], xin, w_zr[...], side_by_side(w_q))
        for s, m, h in zip(slots, motion, hidden):
            motion_out[s] = m
            hid[s] = h
            hid_first[s] = h[:WIDTH].astype(BF16)
            hid_last[s] = h[2 * WIDTH :].astype(BF16)
        add_messages(acc, idx, slots, hidden, w_msg[...])
        return carry

    lax.fori_loop(0, (count + 1) // 2, body, 0)
    give_sums(acc, part, part_other)


def second_kernel(
    table, flags, s0, s1, motion, hid, first, second, w_zr, w_q, w_msg,
    part, part_other, state_buf, acc, idx,
):
    count = read_table(table, idx)
    acc[...] = jnp.zeros_like(acc)

    def body(i, carry):
        slots = [2 * i + j for j in range(2)]
        for j, s in enumerate(slots):
            source = jnp.maximum(idx[s], 0) // SLOTS
            for k, piece in enumerate((s0, s1)):

                @pl.when(source // 4 == k)
                def _():
                    state_buf[j] = piece[source % 4]

        state = [state_buf[j].reshape(WIDE, CHANS).astype(F32) for j in range(2)]
        xin = [(motion[s].astype(F32) + c).astype(BF16) for s, c in zip(slots, state)]
        hidden = []
        for s in slots:
            above, below = arrived(flags, first[SLOTS + s].astype(F32), second[SLOTS + s].astype(F32))
            hidden.append(jnp.concatenate([above, hid[s], below]))
        hidden = gru(hidden, xin, w_zr[...], side_by_side(w_q))
        add_messages(acc, idx, slots, hidden, w_msg[...])
        return carry

    lax.fori_loop(0, (count + 1) // 2, body, 0)
    give_sums(acc, part, part_other)


def arrived(flags, first, second):
    weight = [flags[k : k + 1].astype(first.dtype) for k in range(4)]
    return first * weight[0] + second * weight[1], first * weight[2] + second * weight[3]


def state_kernel(flags, own, near, upd, first, second, w_res, out):
    for half, piece in enumerate((own, near)):
        fields = []
        for frame in (2 * half, 2 * half + 1):
            rows = pl.ds(2 * frame, 2)
            above, below = arrived(flags, first[rows].reshape(2 * WIDTH, CHANS), second[rows].reshape(2 * WIDTH, CHANS))
            fields.append(jnp.concatenate([above, upd[frame].reshape(OWN, CHANS), below]))
        new = conv_rows(fields, side_by_side(w_res), 5).reshape(2, 5, WIDTH, CHANS)
        new = (piece[:, 11:16].astype(F32) + new).astype(BF16)
        out[2 * half : 2 * half + 2, 1:4] = new[:, 1:4]
        out[2 * half : 2 * half + 2, 0] = new[:, 0] * flags[4:5].astype(BF16)
        out[2 * half : 2 * half + 2, 4] = new[:, 4] * flags[5:6].astype(BF16)


def last_kernel(flags, state, upd, first, second, w_res, out):
    fields = []
    for frame in range(2):
        above, below = arrived(flags, first[frame, 0], second[frame, 0])
        fields.append(jnp.concatenate([above, upd[frame].reshape(OWN, CHANS), below]))
    new = conv_rows(fields, side_by_side(w_res), ROWS).reshape(2, ROWS, WIDTH, CHANS)
    out[...] = (state[:2, 1:4].astype(F32) + new).astype(BF16)


VM = pl.BlockSpec(memory_space=pltpu.VMEM)


def call(kernel, outs, scratch, flops, *args):
    size = sum(a.size * a.dtype.itemsize for a in args)
    return pl.pallas_call(
        kernel,
        out_shape=outs,
        in_specs=[VM] * len(args),
        out_specs=[VM] * len(outs),
        scratch_shapes=scratch,
        compiler_params=pltpu.CompilerParams(vmem_limit_bytes=14 * 2**20),
        cost_estimate=pl.CostEstimate(flops=flops, bytes_accessed=size, transcendentals=0),
    )(*args)


def slot_table(pairs, index):
    chip, core = index >> 1, index & 1
    sources, targets, owners = (pairs[:, k] for k in range(3))

    def place(frame):
        dev = (frame >> 1) - 2 * chip
        other = jnp.where((dev >= 1) != (core == 1), 4, 0)
        return other + jnp.where((dev < 0) | (dev > 1), 2, 0) + (frame & 1)

    mine = (owners >> 1) == chip
    order = jnp.arange(pairs.shape[0], dtype=jnp.int32)
    ranks = jnp.sum(jnp.where((order[None, :] < order[:, None]) & mine[None, :], 1, 0), axis=1)
    codes = place(sources) * SLOTS + place(targets)
    levels = 2 * jnp.arange(SLOTS, dtype=jnp.int32) + core
    picked = jnp.where((ranks[None, :] == levels[:, None]) & mine[None, :], codes[None, :] + 1, 0)
    picked = jnp.sum(picked, axis=1) - 1
    return picked[None]


def row_flags(row):
    line = lax.broadcasted_iota(jnp.int32, (8, CHANS), 0)
    odd, up, down = row % 2 == 1, row > 0, row < 3
    flags = ((line == 0) & (up & odd)) | ((line == 1) & (up & ~odd)) | ((line == 2) & (down & ~odd))
    flags = flags | ((line == 3) & (down & odd)) | ((line == 4) & up) | ((line == 5) & down)
    return flags.astype(F32)


def local(fmap, context, pairs, w_corr, w_zr, w_q, w_msg, w_res):
    index, row = lax.axis_index("frames"), lax.axis_index("rows")
    n_frames, n_rows = lax.axis_size("frames"), lax.axis_size("rows")
    even_swap = [(i, i ^ 1) for i in range(n_rows)]
    odd_swap = [(i, n_rows - 1 - i) for i in range(n_rows)]
    odd = row % 2 == 1
    across = [(i, (i + 2) % 4) for i in range(n_rows)]
    core_swap = [(i, i ^ 1) for i in range(n_frames)]
    partner = {i: i + 1 if i % 2 else i - 1 for i in range(1, n_frames - 1)}
    chip_swap = [
        (i * n_rows + j, partner[i] * n_rows + j if i in partner else i * n_rows + (j ^ 1))
        for i in range(n_frames)
        for j in range(n_rows)
    ]

    def rows_swaps(to_above, to_below):
        first = lax.ppermute(jnp.where(odd, to_above, to_below), "rows", even_swap)
        second = lax.ppermute(jnp.where(odd, to_below, to_above), "rows", odd_swap)
        return first, second

    def swap_core(x):
        return lax.ppermute(x, "frames", core_swap)

    def swap_chip(x):
        return lax.ppermute(x, ("frames", "rows"), chip_swap)

    with jax.named_scope("feature_rows"):
        far = lax.ppermute(jnp.where(row < 2, fmap[:, 2:], fmap[:, :1]), "rows", across)
        first, second = rows_swaps(
            jnp.concatenate([fmap, context[:, :1]], axis=1), jnp.concatenate([fmap, context[:, 2:]], axis=1)
        )
        none = jnp.zeros_like(far)
        blank = jnp.zeros_like(first)
        from_above = jnp.where(row > 0, jnp.where(odd, first, second), blank)
        from_below = jnp.where(row < n_rows - 1, jnp.where(odd, second, first), blank)
        own = jnp.concatenate(
            [
                jnp.where(row < 2, none, far),
                from_above[:, :3],
                fmap,
                from_below[:, :3],
                jnp.where(row < 2, far, none),
                from_above[:, 3:],
                context,
                from_below[:, 3:],
            ],
            axis=1,
        )
    own, pairs = lax.optimization_barrier((own, pairs))
    idx, flags = slot_table(pairs, index), row_flags(row)
    with jax.named_scope("feature_window"):
        near = swap_chip(own)
        own_other = swap_core(own)
        near_other = swap_core(near)

    with jax.named_scope("first_iteration"):
        sums = [jax.ShapeDtypeStruct((4, OWN, CHANS), BF16)] * 2
        edge_rows = [jax.ShapeDtypeStruct((SLOTS, WIDTH, CHANS), BF16)] * 2
        part, part_other, hid, hid_first, hid_last, motion = call(
            first_kernel,
            [
                *sums,
                jax.ShapeDtypeStruct((SLOTS, OWN, CHANS), F32),
                *edge_rows,
                jax.ShapeDtypeStruct((SLOTS, WIDE, CHANS), BF16),
            ],
            [
                pltpu.VMEM((2, 5, WIDTH, CHANS), BF16),
                pltpu.VMEM((2, 11, WIDTH, CHANS), BF16),
                pltpu.VMEM((2, 5, WIDTH, CHANS), BF16),
                pltpu.VMEM((SLOTS, OWN, CHANS), F32),
                pltpu.VMEM((WIDTH, WIDTH), BF16),
                pltpu.VMEM((CHANS, CHANS), BF16),
                pltpu.VMEM((WIDTH, CHANS), F32),
                pltpu.SMEM((SLOTS,), jnp.int32),
            ],
            2_000_000_000,
            idx, own, near, own_other, near_other, w_corr, w_zr, w_q, w_msg,
        )

    with jax.named_scope("first_sums"):
        mine = part.astype(F32) + swap_core(part_other).astype(F32)
        sent = mine.astype(BF16)
        arrived = swap_chip(sent).astype(F32)
        total = mine + jnp.concatenate([arrived[2:], arrived[:2]])
        upd = jnp.maximum(total, 0.0).astype(BF16).reshape(4, ROWS, WIDTH, CHANS)
    with jax.named_scope("update_rows"):
        first, second = rows_swaps(
            jnp.concatenate([upd[:, :2].reshape(8, WIDTH, CHANS), hid_first]),
            jnp.concatenate([upd[:, 1:].reshape(8, WIDTH, CHANS), hid_last]),
        )
    with jax.named_scope("first_state"):
        [state] = call(
            state_kernel,
            [jax.ShapeDtypeStruct((4, 5, WIDTH, CHANS), BF16)],
            [],
            400_000_000,
            flags, own, near, upd, first, second, w_res,
        )
        state_other = swap_core(state)
    with jax.named_scope("second_iteration"):
        part, part_other = call(
            second_kernel,
            sums,
            [
                pltpu.VMEM((2, 5, WIDTH, CHANS), BF16),
                pltpu.VMEM((SLOTS, OWN, CHANS), F32),
                pltpu.SMEM((SLOTS,), jnp.int32),
            ],
            1_500_000_000,
            idx, flags, state, state_other, motion, hid, first, second, w_zr, w_q, w_msg,
        )
    with jax.named_scope("second_sums"):
        mine = part.astype(F32) + swap_core(part_other).astype(F32)
        arrived = swap_chip(mine[2:].astype(BF16)).astype(F32)
        upd = jnp.maximum(mine[:2] + arrived, 0.0).astype(BF16).reshape(2, ROWS, WIDTH, CHANS)
        first, second = rows_swaps(upd[:, :1], upd[:, 2:])
    with jax.named_scope("last_state"):
        [out] = call(
            last_kernel,
            [jax.ShapeDtypeStruct((2, ROWS, WIDTH, CHANS), BF16)],
            [],
            120_000_000,
            flags, state, upd, first, second, w_res,
        )
    return out


def solution(mesh):
    placed = (
        P("frames", "rows", None, None),
        P("frames", "rows", None, None),
        P(),
        P(),
        P(),
        P(),
        P(),
        P(),
    )
    return jax.shard_map(
        local,
        mesh=mesh,
        in_specs=placed,
        out_specs=P("frames", "rows", None, None),
        check_vma=False,
    )
```

```python
import jax
import jax.numpy as jnp
from jax import lax
from jax.experimental import pallas as pl
from jax.experimental.pallas import tpu as pltpu
from jax.sharding import PartitionSpec as P

SLOTS = 8
ROWS = 3
WIDTH = 64
CHANS = 128
SPAN = 7
WIDE = 5 * WIDTH
OWN = ROWS * WIDTH
F32 = jnp.float32
BF16 = jnp.bfloat16


def dot(a, b):
    return lax.dot_general(a, b, (((1,), (0,)), ((), ())), preferred_element_type=F32)


def dot_t(a, b):
    return lax.dot_general(a, b, (((1,), (1,)), ((), ())), preferred_element_type=F32)


def sigmoid(x):
    return 0.5 * jnp.tanh(0.5 * x) + 0.5


def side_by_side(weights):
    rows = [jnp.concatenate([weights[3 * k + j] for j in range(3)], axis=1) for k in range(3)]
    return jnp.concatenate(rows, axis=0)


def conv_rows(fields, weights, rows):
    size = rows * WIDTH
    taps = [
        jnp.concatenate([field[k * WIDTH : k * WIDTH + size] for k in range(3)], axis=1) for field in fields
    ]
    out = dot(jnp.concatenate(taps), weights)
    size *= len(fields)
    column = lax.broadcasted_iota(jnp.int32, (size, CHANS), 0) & (WIDTH - 1)
    left = jnp.where(column == 0, 0.0, pltpu.roll(out[:, :CHANS], 1, 0))
    right = jnp.where(column == WIDTH - 1, 0.0, pltpu.roll(out[:, 2 * CHANS :], size - 1, 0))
    return out[:, CHANS : 2 * CHANS] + left + right


def gru(hidden, xin, w_zr, w_q):
    joined = [jnp.concatenate([h.astype(BF16), x], axis=1) for h, x in zip(hidden, xin)]
    own = slice(WIDTH, WIDTH + OWN)
    reset = sigmoid(dot(jnp.concatenate(joined), w_zr[:, CHANS:]))
    update = sigmoid(dot(jnp.concatenate([j[own] for j in joined]), w_zr[:, :CHANS]))
    gated = (reset * jnp.concatenate(hidden)).astype(BF16)
    fields = [jnp.concatenate([gated[k * WIDE : (k + 1) * WIDE], x], axis=1) for k, x in enumerate(xin)]
    candidate = jnp.tanh(conv_rows(fields, w_q, ROWS))
    old = jnp.concatenate([h[own] for h in hidden])
    new = old + update * (candidate - old)
    return [new[k * OWN : (k + 1) * OWN] for k in range(len(xin))]


def read_table(table, idx):
    count = 0
    for s in range(SLOTS):
        code = table[0, s]
        idx[s] = code
        count += jnp.where(code >= 0, 1, 0)
    return count


def add_messages(acc, idx, slots, hidden, w_msg):
    messages = dot(jnp.concatenate(hidden).astype(BF16), w_msg)
    for k, s in enumerate(slots):

        @pl.when(idx[s] >= 0)
        def _():
            acc[idx[s] // SLOTS] += messages[k * OWN : (k + 1) * OWN, :CHANS]
            acc[idx[s] % SLOTS] += messages[k * OWN : (k + 1) * OWN, CHANS:]


def give_sums(acc, part, part_other):
    part[...] = acc[:4].astype(BF16)
    part_other[...] = acc[4:].astype(BF16)


def first_kernel(
    table, c0, c1, c23, h0, h1, h2, h3, w_corr, w_zr, w_q, w_msg,
    part, part_other, hid, hid_first, hid_last, motion_out,
    feat, rim, ctx, acc, flip, spread, edge, idx,
):
    pieces = ((c0, 0, h0), (c1, 0, h1), (c23, 0, h2), (c23, 2, h3))
    count = read_table(table, idx)
    acc[...] = jnp.zeros_like(acc)
    ends = [lax.broadcasted_iota(jnp.int32, (WIDTH, WIDTH), k) for k in range(2)]
    flip[...] = jnp.where(ends[0] + ends[1] == WIDTH - 1, 1.0, 0.0).astype(BF16)
    lane, tap = [lax.broadcasted_iota(jnp.int32, (CHANS, SPAN * SPAN), k) for k in range(2)]
    place = (lane & (WIDTH - 1)) - 4
    shift = jnp.where(lane < WIDTH, 2 * (place >> 3), jnp.minimum(2 * (place >> 3) + 1, SPAN - 1))
    wanted = (place >= 0) & (place < 32) & ((place & 7) < SPAN) & (tap == SPAN * shift + (place & 7))
    spread[...] = dot(jnp.where(wanted, 1.0, 0.0).astype(BF16), w_corr[...]).astype(BF16)
    column = WIDTH - 1 - lax.broadcasted_iota(jnp.int32, (WIDTH, CHANS), 0)
    lane = lax.broadcasted_iota(jnp.int32, (WIDTH, CHANS), 1)
    place = (lane & (WIDTH - 1)) - 4
    at = column + (place & 7) - 3
    inside = (place >= 0) & (place < 32) & ((place & 7) < SPAN) & (at >= 0) & (at < WIDTH)
    inside = inside & ((place < 24) | (lane >= WIDTH))
    edge[...] = jnp.where(inside, 1.0 / CHANS**0.5, 0.0)
    place = (lax.broadcasted_iota(jnp.int32, (WIDTH, CHANS), 1) & (WIDTH - 1)) - 4

    def body(i, carry):
        slots = [2 * i + j for j in range(2)]
        for j, s in enumerate(slots):
            code = jnp.maximum(idx[s], 0)
            source, target = code // SLOTS, code % SLOTS
            for k, (center, first, halo) in enumerate(pieces):

                @pl.when(source // 2 == k)
                def _():
                    frame = source % 2
                    feat[j, 0], ctx[j, 0] = halo[frame, 3], halo[frame, 8]
                    feat[j, 1:4], ctx[j, 1:4] = center[first + frame, 0:3], center[first + frame, 3:6]
                    feat[j, 4], ctx[j, 4] = halo[frame, 4], halo[frame, 9]

                @pl.when(target // 2 == k)
                def _():
                    frame = target % 2
                    rim[j, 0:4] = halo[frame, 0:4]
                    rim[j, 4:7] = center[first + frame, 0:3]
                    rim[j, 7:11] = halo[frame, 4:8]

        rows = [(j, y) for j in range(2) for y in range(5)]
        turned = dot(flip[...], jnp.concatenate([feat[j, y] for j, y in rows], axis=1)).astype(BF16)
        corr = []
        for j in range(2):
            near = [turned[:, (5 * j + y) * CHANS : (5 * j + y + 1) * CHANS] for y in range(5)]
            totals = [None] * 5
            for t in range(10):
                far = rim[j, t : t + 2].reshape(2 * WIDTH, CHANS)
                uses = [(t - 2 * g, g) for g in range(3) if 0 <= t - 2 * g < 5]
                uses += [(t - 5, 3)] if t >= 5 else []
                table = dot_t(jnp.concatenate([near[y] for y, _ in uses]), far)
                for k, (y, g) in enumerate(uses):
                    part_table = table[k * WIDTH : (k + 1) * WIDTH]
                    moved = pltpu.roll(part_table, 8 * g + 72, 1, stride=1, stride_axis=0)
                    totals[y] = moved if g == 0 else jnp.where(place < 8 * g, totals[y], moved)
            corr += [(total * edge[...]).astype(BF16) for total in totals]
        turned = dot(flip[...], jnp.concatenate(corr, axis=1)).astype(BF16)
        corr = jnp.concatenate([turned[:, k * CHANS : (k + 1) * CHANS] for k in range(len(rows))])
        motion = jnp.maximum(dot(corr, spread[...]), 0.0).astype(BF16)
        motion = [motion[j * WIDE : (j + 1) * WIDE] for j in range(2)]
        state = [ctx[j].reshape(WIDE, CHANS).astype(F32) for j in range(2)]
        xin = [(m.astype(F32) + c).astype(BF16) for m, c in zip(motion, state)]
        hidden = gru([jnp.tanh(c) for c in state], xin, w_zr[...], side_by_side(w_q))
        for s, m, h in zip(slots, motion, hidden):
            motion_out[s] = m
            hid[s] = h
            hid_first[s] = h[:WIDTH].astype(BF16)
            hid_last[s] = h[2 * WIDTH :].astype(BF16)
        add_messages(acc, idx, slots, hidden, w_msg[...])
        return carry

    lax.fori_loop(0, (count + 1) // 2, body, 0)
    give_sums(acc, part, part_other)


def second_kernel(
    table, flags, s0, s1, motion, hid, first, second, w_zr, w_q, w_msg,
    part, part_other, state_buf, acc, idx,
):
    count = read_table(table, idx)
    acc[...] = jnp.zeros_like(acc)

    def body(i, carry):
        slots = [2 * i + j for j in range(2)]
        for j, s in enumerate(slots):
            source = jnp.maximum(idx[s], 0) // SLOTS
            for k, piece in enumerate((s0, s1)):

                @pl.when(source // 4 == k)
                def _():
                    state_buf[j] = piece[source % 4]

        state = [state_buf[j].reshape(WIDE, CHANS).astype(F32) for j in range(2)]
        xin = [(motion[s].astype(F32) + c).astype(BF16) for s, c in zip(slots, state)]
        hidden = []
        for s in slots:
            above, below = arrived(flags, first[SLOTS + s].astype(F32), second[SLOTS + s].astype(F32))
            hidden.append(jnp.concatenate([above, hid[s], below]))
        hidden = gru(hidden, xin, w_zr[...], side_by_side(w_q))
        add_messages(acc, idx, slots, hidden, w_msg[...])
        return carry

    lax.fori_loop(0, (count + 1) // 2, body, 0)
    give_sums(acc, part, part_other)


def arrived(flags, first, second):
    weight = [flags[k : k + 1].astype(first.dtype) for k in range(4)]
    return first * weight[0] + second * weight[1], first * weight[2] + second * weight[3]


def state_kernel(flags, c0, c1, h0, h1, upd, first, second, w_res, out):
    for half, (center, halo) in enumerate(((c0, h0), (c1, h1))):
        fields = []
        for frame in (2 * half, 2 * half + 1):
            rows = pl.ds(2 * frame, 2)
            above, below = arrived(flags, first[rows].reshape(2 * WIDTH, CHANS), second[rows].reshape(2 * WIDTH, CHANS))
            fields.append(jnp.concatenate([above, upd[frame].reshape(OWN, CHANS), below]))
        new = conv_rows(fields, side_by_side(w_res), 5).reshape(2, 5, WIDTH, CHANS)
        base = jnp.concatenate([halo[:, 8:9], center[:, 3:6], halo[:, 9:10]], axis=1)
        new = (base.astype(F32) + new).astype(BF16)
        out[2 * half : 2 * half + 2, 1:4] = new[:, 1:4]
        out[2 * half : 2 * half + 2, 0] = new[:, 0] * flags[4:5].astype(BF16)
        out[2 * half : 2 * half + 2, 4] = new[:, 4] * flags[5:6].astype(BF16)


def last_kernel(flags, state, upd, first, second, w_res, out):
    fields = []
    for frame in range(2):
        above, below = arrived(flags, first[frame, 0], second[frame, 0])
        fields.append(jnp.concatenate([above, upd[frame].reshape(OWN, CHANS), below]))
    new = conv_rows(fields, side_by_side(w_res), ROWS).reshape(2, ROWS, WIDTH, CHANS)
    out[...] = (state[:2, 1:4].astype(F32) + new).astype(BF16)


VM = pl.BlockSpec(memory_space=pltpu.VMEM)


def call(kernel, outs, scratch, flops, *args):
    size = sum(a.size * a.dtype.itemsize for a in args)
    return pl.pallas_call(
        kernel,
        out_shape=outs,
        in_specs=[VM] * len(args),
        out_specs=[VM] * len(outs),
        scratch_shapes=scratch,
        compiler_params=pltpu.CompilerParams(vmem_limit_bytes=14 * 2**20),
        cost_estimate=pl.CostEstimate(flops=flops, bytes_accessed=size, transcendentals=0),
    )(*args)


def slot_table(pairs, index):
    chip, core = index >> 1, index & 1
    sources, targets, owners = (pairs[:, k] for k in range(3))

    def place(frame):
        dev = (frame >> 1) - 2 * chip
        other = jnp.where((dev >= 1) != (core == 1), 4, 0)
        return other + jnp.where((dev < 0) | (dev > 1), 2, 0) + (frame & 1)

    mine = (owners >> 1) == chip
    order = jnp.arange(pairs.shape[0], dtype=jnp.int32)
    ranks = jnp.sum(jnp.where((order[None, :] < order[:, None]) & mine[None, :], 1, 0), axis=1)
    codes = place(sources) * SLOTS + place(targets)
    levels = 2 * jnp.arange(SLOTS, dtype=jnp.int32) + core
    picked = jnp.where((ranks[None, :] == levels[:, None]) & mine[None, :], codes[None, :] + 1, 0)
    picked = jnp.sum(picked, axis=1) - 1
    return picked[None]


def row_flags(row):
    line = lax.broadcasted_iota(jnp.int32, (8, CHANS), 0)
    odd, up, down = row % 2 == 1, row > 0, row < 3
    flags = ((line == 0) & (up & odd)) | ((line == 1) & (up & ~odd)) | ((line == 2) & (down & ~odd))
    flags = flags | ((line == 3) & (down & odd)) | ((line == 4) & up) | ((line == 5) & down)
    return flags.astype(F32)


def local(fmap, context, pairs, w_corr, w_zr, w_q, w_msg, w_res):
    index, row = lax.axis_index("frames"), lax.axis_index("rows")
    n_frames, n_rows = lax.axis_size("frames"), lax.axis_size("rows")
    even_swap = [(i, i ^ 1) for i in range(n_rows)]
    odd_swap = [(i, n_rows - 1 - i) for i in range(n_rows)]
    odd = row % 2 == 1
    across = [(i, (i + 2) % 4) for i in range(n_rows)]
    core_swap = [(i, i ^ 1) for i in range(n_frames)]
    partner = {i: i + 1 if i % 2 else i - 1 for i in range(1, n_frames - 1)}
    chip_swap = [
        (i * n_rows + j, partner[i] * n_rows + j if i in partner else i * n_rows + (j ^ 1))
        for i in range(n_frames)
        for j in range(n_rows)
    ]

    def rows_swaps(to_above, to_below):
        first = lax.ppermute(jnp.where(odd, to_above, to_below), "rows", even_swap)
        second = lax.ppermute(jnp.where(odd, to_below, to_above), "rows", odd_swap)
        return first, second

    def swap_core(x):
        return lax.ppermute(x, "frames", core_swap)

    def swap_chip(x):
        return lax.ppermute(x, ("frames", "rows"), chip_swap)

    with jax.named_scope("feature_rows"):
        center = jnp.concatenate([fmap, context], axis=1)
        near_center = swap_chip(center)
        far = lax.ppermute(jnp.where(row < 2, fmap[:, 2:], fmap[:, :1]), "rows", across)
        first, second = rows_swaps(
            jnp.concatenate([fmap, context[:, :1]], axis=1), jnp.concatenate([fmap, context[:, 2:]], axis=1)
        )
        none = jnp.zeros_like(far)
        blank = jnp.zeros_like(first)
        from_above = jnp.where(row > 0, jnp.where(odd, first, second), blank)
        from_below = jnp.where(row < n_rows - 1, jnp.where(odd, second, first), blank)
        halo = jnp.concatenate(
            [
                jnp.where(row < 2, none, far),
                from_above[:, :3],
                from_below[:, :3],
                jnp.where(row < 2, far, none),
                from_above[:, 3:],
                from_below[:, 3:],
            ],
            axis=1,
        )
    halo, pairs = lax.optimization_barrier((halo, pairs))
    idx, flags = slot_table(pairs, index), row_flags(row)
    with jax.named_scope("feature_window"):
        near_halo = swap_chip(halo)
        halo_other = swap_core(halo)
        center_other = swap_core(jnp.concatenate([center, near_center]))
        near_halo_other = swap_core(near_halo)

    with jax.named_scope("first_iteration"):
        sums = [jax.ShapeDtypeStruct((4, OWN, CHANS), BF16)] * 2
        edge_rows = [jax.ShapeDtypeStruct((SLOTS, WIDTH, CHANS), BF16)] * 2
        part, part_other, hid, hid_first, hid_last, motion = call(
            first_kernel,
            [
                *sums,
                jax.ShapeDtypeStruct((SLOTS, OWN, CHANS), F32),
                *edge_rows,
                jax.ShapeDtypeStruct((SLOTS, WIDE, CHANS), BF16),
            ],
            [
                pltpu.VMEM((2, 5, WIDTH, CHANS), BF16),
                pltpu.VMEM((2, 11, WIDTH, CHANS), BF16),
                pltpu.VMEM((2, 5, WIDTH, CHANS), BF16),
                pltpu.VMEM((SLOTS, OWN, CHANS), F32),
                pltpu.VMEM((WIDTH, WIDTH), BF16),
                pltpu.VMEM((CHANS, CHANS), BF16),
                pltpu.VMEM((WIDTH, CHANS), F32),
                pltpu.SMEM((SLOTS,), jnp.int32),
            ],
            2_000_000_000,
            idx, center, near_center, center_other, halo, near_halo, halo_other, near_halo_other, w_corr, w_zr, w_q, w_msg,
        )

    with jax.named_scope("first_sums"):
        mine = part.astype(F32) + swap_core(part_other).astype(F32)
        sent = mine.astype(BF16)
        arrived = swap_chip(sent).astype(F32)
        total = mine + jnp.concatenate([arrived[2:], arrived[:2]])
        upd = jnp.maximum(total, 0.0).astype(BF16).reshape(4, ROWS, WIDTH, CHANS)
    with jax.named_scope("update_rows"):
        first, second = rows_swaps(
            jnp.concatenate([upd[:, :2].reshape(8, WIDTH, CHANS), hid_first]),
            jnp.concatenate([upd[:, 1:].reshape(8, WIDTH, CHANS), hid_last]),
        )
    with jax.named_scope("first_state"):
        [state] = call(
            state_kernel,
            [jax.ShapeDtypeStruct((4, 5, WIDTH, CHANS), BF16)],
            [],
            400_000_000,
            flags, center, near_center, halo, near_halo, upd, first, second, w_res,
        )
        state_other = swap_core(state)
    with jax.named_scope("second_iteration"):
        part, part_other = call(
            second_kernel,
            sums,
            [
                pltpu.VMEM((2, 5, WIDTH, CHANS), BF16),
                pltpu.VMEM((SLOTS, OWN, CHANS), F32),
                pltpu.SMEM((SLOTS,), jnp.int32),
            ],
            1_500_000_000,
            idx, flags, state, state_other, motion, hid, first, second, w_zr, w_q, w_msg,
        )
    with jax.named_scope("second_sums"):
        mine = part.astype(F32) + swap_core(part_other).astype(F32)
        arrived = swap_chip(mine[2:].astype(BF16)).astype(F32)
        upd = jnp.maximum(mine[:2] + arrived, 0.0).astype(BF16).reshape(2, ROWS, WIDTH, CHANS)
        first, second = rows_swaps(upd[:, :1], upd[:, 2:])
    with jax.named_scope("last_state"):
        [out] = call(
            last_kernel,
            [jax.ShapeDtypeStruct((2, ROWS, WIDTH, CHANS), BF16)],
            [],
            120_000_000,
            flags, state, upd, first, second, w_res,
        )
    return out


def solution(mesh):
    placed = (
        P("frames", "rows", None, None),
        P("frames", "rows", None, None),
        P(),
        P(),
        P(),
        P(),
        P(),
        P(),
    )
    return jax.shard_map(
        local,
        mesh=mesh,
        in_specs=placed,
        out_specs=P("frames", "rows", None, None),
        check_vma=False,
    )
```

```python
import jax
import jax.numpy as jnp
from jax import lax
from jax.experimental import pallas as pl
from jax.experimental.pallas import tpu as pltpu
from jax.sharding import PartitionSpec as P

SLOTS = 8
ROWS = 3
WIDTH = 64
CHANS = 128
SPAN = 7
WIDE = 5 * WIDTH
OWN = ROWS * WIDTH
F32 = jnp.float32
BF16 = jnp.bfloat16


def dot(a, b):
    return lax.dot_general(a, b, (((1,), (0,)), ((), ())), preferred_element_type=F32)


def dot_t(a, b):
    return lax.dot_general(a, b, (((1,), (1,)), ((), ())), preferred_element_type=F32)


def sigmoid(x):
    return 0.5 * jnp.tanh(0.5 * x) + 0.5


def side_by_side(weights):
    rows = [jnp.concatenate([weights[3 * k + j] for j in range(3)], axis=1) for k in range(3)]
    return jnp.concatenate(rows, axis=0)


def conv_rows(fields, weights, rows):
    size = rows * WIDTH
    taps = [
        jnp.concatenate([field[k * WIDTH : k * WIDTH + size] for k in range(3)], axis=1) for field in fields
    ]
    out = dot(jnp.concatenate(taps), weights)
    size *= len(fields)
    column = lax.broadcasted_iota(jnp.int32, (size, CHANS), 0) & (WIDTH - 1)
    left = jnp.where(column == 0, 0.0, pltpu.roll(out[:, :CHANS], 1, 0))
    right = jnp.where(column == WIDTH - 1, 0.0, pltpu.roll(out[:, 2 * CHANS :], size - 1, 0))
    return out[:, CHANS : 2 * CHANS] + left + right


def gru(hidden, xin, w_zr, w_q):
    joined = [jnp.concatenate([h.astype(BF16), x], axis=1) for h, x in zip(hidden, xin)]
    own = slice(WIDTH, WIDTH + OWN)
    reset = sigmoid(dot(jnp.concatenate(joined), w_zr[:, CHANS:]))
    update = sigmoid(dot(jnp.concatenate([j[own] for j in joined]), w_zr[:, :CHANS]))
    gated = (reset * jnp.concatenate(hidden)).astype(BF16)
    fields = [jnp.concatenate([gated[k * WIDE : (k + 1) * WIDE], x], axis=1) for k, x in enumerate(xin)]
    candidate = jnp.tanh(conv_rows(fields, w_q, ROWS))
    old = jnp.concatenate([h[own] for h in hidden])
    new = old + update * (candidate - old)
    return [new[k * OWN : (k + 1) * OWN] for k in range(len(xin))]


def read_table(table, idx):
    count = 0
    for s in range(SLOTS):
        code = table[0, s]
        idx[s] = code
        count += jnp.where(code >= 0, 1, 0)
    return count


def add_messages(acc, idx, slots, hidden, w_msg):
    messages = dot(jnp.concatenate(hidden).astype(BF16), w_msg)
    for k, s in enumerate(slots):

        @pl.when(idx[s] >= 0)
        def _():
            acc[idx[s] // SLOTS] += messages[k * OWN : (k + 1) * OWN, :CHANS]
            acc[idx[s] % SLOTS] += messages[k * OWN : (k + 1) * OWN, CHANS:]


def give_sums(acc, part, part_other):
    part[...] = acc[:4].astype(BF16)
    part_other[...] = acc[4:].astype(BF16)


def first_kernel(
    table, c0, c1, c23, h0, h1, h2, h3, w_corr, w_zr, w_q, w_msg,
    part, part_other, hid, hid_first, hid_last, motion_out, base,
    feat, rim, ctx, acc, flip, spread, edge, idx,
):
    pieces = ((c0, 0, h0), (c1, 0, h1), (c23, 0, h2), (c23, 2, h3))
    count = read_table(table, idx)
    acc[...] = jnp.zeros_like(acc)
    for half, (center, _, halo) in enumerate(pieces[:2]):
        frames = pl.ds(2 * half, 2)
        base[frames, 0], base[frames, 1:4], base[frames, 4] = halo[:, 8], center[:, 3:6], halo[:, 9]
    ends = [lax.broadcasted_iota(jnp.int32, (WIDTH, WIDTH), k) for k in range(2)]
    flip[...] = jnp.where(ends[0] + ends[1] == WIDTH - 1, 1.0, 0.0).astype(BF16)
    lane, tap = [lax.broadcasted_iota(jnp.int32, (CHANS, SPAN * SPAN), k) for k in range(2)]
    place = (lane & (WIDTH - 1)) - 4
    shift = jnp.where(lane < WIDTH, 2 * (place >> 3), jnp.minimum(2 * (place >> 3) + 1, SPAN - 1))
    wanted = (place >= 0) & (place < 32) & ((place & 7) < SPAN) & (tap == SPAN * shift + (place & 7))
    spread[...] = dot(jnp.where(wanted, 1.0, 0.0).astype(BF16), w_corr[...]).astype(BF16)
    column = WIDTH - 1 - lax.broadcasted_iota(jnp.int32, (WIDTH, CHANS), 0)
    lane = lax.broadcasted_iota(jnp.int32, (WIDTH, CHANS), 1)
    place = (lane & (WIDTH - 1)) - 4
    at = column + (place & 7) - 3
    inside = (place >= 0) & (place < 32) & ((place & 7) < SPAN) & (at >= 0) & (at < WIDTH)
    inside = inside & ((place < 24) | (lane >= WIDTH))
    edge[...] = jnp.where(inside, 1.0 / CHANS**0.5, 0.0)
    place = (lax.broadcasted_iota(jnp.int32, (WIDTH, CHANS), 1) & (WIDTH - 1)) - 4

    def body(i, carry):
        slots = [2 * i + j for j in range(2)]
        for j, s in enumerate(slots):
            code = jnp.maximum(idx[s], 0)
            source, target = code // SLOTS, code % SLOTS
            for k, (center, first, halo) in enumerate(pieces):

                @pl.when(source // 2 == k)
                def _():
                    frame = source % 2
                    feat[j, 0], ctx[j, 0] = halo[frame, 3], halo[frame, 8]
                    feat[j, 1:4], ctx[j, 1:4] = center[first + frame, 0:3], center[first + frame, 3:6]
                    feat[j, 4], ctx[j, 4] = halo[frame, 4], halo[frame, 9]

                @pl.when(target // 2 == k)
                def _():
                    frame = target % 2
                    rim[j, 0:4] = halo[frame, 0:4]
                    rim[j, 4:7] = center[first + frame, 0:3]
                    rim[j, 7:11] = halo[frame, 4:8]

        rows = [(j, y) for j in range(2) for y in range(5)]
        turned = dot(flip[...], jnp.concatenate([feat[j, y] for j, y in rows], axis=1)).astype(BF16)
        corr = []
        for j in range(2):
            near = [turned[:, (5 * j + y) * CHANS : (5 * j + y + 1) * CHANS] for y in range(5)]
            totals = [None] * 5
            for t in range(10):
                far = rim[j, t : t + 2].reshape(2 * WIDTH, CHANS)
                uses = [(t - 2 * g, g) for g in range(3) if 0 <= t - 2 * g < 5]
                uses += [(t - 5, 3)] if t >= 5 else []
                table = dot_t(jnp.concatenate([near[y] for y, _ in uses]), far)
                for k, (y, g) in enumerate(uses):
                    part_table = table[k * WIDTH : (k + 1) * WIDTH]
                    moved = pltpu.roll(part_table, 8 * g + 72, 1, stride=1, stride_axis=0)
                    totals[y] = moved if g == 0 else jnp.where(place < 8 * g, totals[y], moved)
            corr += [(total * edge[...]).astype(BF16) for total in totals]
        turned = dot(flip[...], jnp.concatenate(corr, axis=1)).astype(BF16)
        corr = jnp.concatenate([turned[:, k * CHANS : (k + 1) * CHANS] for k in range(len(rows))])
        motion = jnp.maximum(dot(corr, spread[...]), 0.0).astype(BF16)
        motion = [motion[j * WIDE : (j + 1) * WIDE] for j in range(2)]
        state = [ctx[j].reshape(WIDE, CHANS).astype(F32) for j in range(2)]
        xin = [(m.astype(F32) + c).astype(BF16) for m, c in zip(motion, state)]
        hidden = gru([jnp.tanh(c) for c in state], xin, w_zr[...], side_by_side(w_q))
        for s, m, h in zip(slots, motion, hidden):
            motion_out[s] = m
            hid[s] = h
            hid_first[s] = h[:WIDTH].astype(BF16)
            hid_last[s] = h[2 * WIDTH :].astype(BF16)
        add_messages(acc, idx, slots, hidden, w_msg[...])
        return carry

    lax.fori_loop(0, (count + 1) // 2, body, 0)
    give_sums(acc, part, part_other)


def second_kernel(
    table, flags, s0, s1, motion, hid, first, second, w_zr, w_q, w_msg,
    part, part_other, state_buf, acc, idx,
):
    count = read_table(table, idx)
    acc[...] = jnp.zeros_like(acc)

    def body(i, carry):
        slots = [2 * i + j for j in range(2)]
        for j, s in enumerate(slots):
            source = jnp.maximum(idx[s], 0) // SLOTS
            for k, piece in enumerate((s0, s1)):

                @pl.when(source // 4 == k)
                def _():
                    state_buf[j] = piece[source % 4]

        state = [state_buf[j].reshape(WIDE, CHANS).astype(F32) for j in range(2)]
        xin = [(motion[s].astype(F32) + c).astype(BF16) for s, c in zip(slots, state)]
        hidden = []
        for s in slots:
            above, below = arrived(flags, first[SLOTS + s].astype(F32), second[SLOTS + s].astype(F32))
            hidden.append(jnp.concatenate([above, hid[s], below]))
        hidden = gru(hidden, xin, w_zr[...], side_by_side(w_q))
        add_messages(acc, idx, slots, hidden, w_msg[...])
        return carry

    lax.fori_loop(0, (count + 1) // 2, body, 0)
    give_sums(acc, part, part_other)


def arrived(flags, first, second):
    weight = [flags[k : k + 1].astype(first.dtype) for k in range(4)]
    return first * weight[0] + second * weight[1], first * weight[2] + second * weight[3]


def state_kernel(flags, base, upd, first, second, w_res, out):
    for half in range(2):
        fields = []
        for frame in (2 * half, 2 * half + 1):
            rows = pl.ds(2 * frame, 2)
            above, below = arrived(flags, first[rows].reshape(2 * WIDTH, CHANS), second[rows].reshape(2 * WIDTH, CHANS))
            fields.append(jnp.concatenate([above, upd[frame].reshape(OWN, CHANS), below]))
        new = conv_rows(fields, side_by_side(w_res), 5).reshape(2, 5, WIDTH, CHANS)
        new = (base[2 * half : 2 * half + 2].astype(F32) + new).astype(BF16)
        out[2 * half : 2 * half + 2, 1:4] = new[:, 1:4]
        out[2 * half : 2 * half + 2, 0] = new[:, 0] * flags[4:5].astype(BF16)
        out[2 * half : 2 * half + 2, 4] = new[:, 4] * flags[5:6].astype(BF16)


def last_kernel(flags, state, upd, first, second, w_res, out):
    fields = []
    for frame in range(2):
        above, below = arrived(flags, first[frame, 0], second[frame, 0])
        fields.append(jnp.concatenate([above, upd[frame].reshape(OWN, CHANS), below]))
    new = conv_rows(fields, side_by_side(w_res), ROWS).reshape(2, ROWS, WIDTH, CHANS)
    out[...] = (state[:2, 1:4].astype(F32) + new).astype(BF16)


VM = pl.BlockSpec(memory_space=pltpu.VMEM)


def call(kernel, outs, scratch, flops, *args):
    size = sum(a.size * a.dtype.itemsize for a in args)
    return pl.pallas_call(
        kernel,
        out_shape=outs,
        in_specs=[VM] * len(args),
        out_specs=[VM] * len(outs),
        scratch_shapes=scratch,
        compiler_params=pltpu.CompilerParams(vmem_limit_bytes=14 * 2**20),
        cost_estimate=pl.CostEstimate(flops=flops, bytes_accessed=size, transcendentals=0),
    )(*args)


def slot_table(pairs, index):
    chip, core = index >> 1, index & 1
    sources, targets, owners = (pairs[:, k] for k in range(3))

    def place(frame):
        dev = (frame >> 1) - 2 * chip
        other = jnp.where((dev >= 1) != (core == 1), 4, 0)
        return other + jnp.where((dev < 0) | (dev > 1), 2, 0) + (frame & 1)

    mine = (owners >> 1) == chip
    order = jnp.arange(pairs.shape[0], dtype=jnp.int32)
    ranks = jnp.sum(jnp.where((order[None, :] < order[:, None]) & mine[None, :], 1, 0), axis=1)
    codes = place(sources) * SLOTS + place(targets)
    levels = 2 * jnp.arange(SLOTS, dtype=jnp.int32) + core
    picked = jnp.where((ranks[None, :] == levels[:, None]) & mine[None, :], codes[None, :] + 1, 0)
    picked = jnp.sum(picked, axis=1) - 1
    return picked[None]


def row_flags(row):
    line = lax.broadcasted_iota(jnp.int32, (8, CHANS), 0)
    odd, up, down = row % 2 == 1, row > 0, row < 3
    flags = ((line == 0) & (up & odd)) | ((line == 1) & (up & ~odd)) | ((line == 2) & (down & ~odd))
    flags = flags | ((line == 3) & (down & odd)) | ((line == 4) & up) | ((line == 5) & down)
    return flags.astype(F32)


def local(fmap, context, pairs, w_corr, w_zr, w_q, w_msg, w_res):
    index, row = lax.axis_index("frames"), lax.axis_index("rows")
    n_frames, n_rows = lax.axis_size("frames"), lax.axis_size("rows")
    even_swap = [(i, i ^ 1) for i in range(n_rows)]
    odd_swap = [(i, n_rows - 1 - i) for i in range(n_rows)]
    odd = row % 2 == 1
    across = [(i, (i + 2) % 4) for i in range(n_rows)]
    core_swap = [(i, i ^ 1) for i in range(n_frames)]
    partner = {i: i + 1 if i % 2 else i - 1 for i in range(1, n_frames - 1)}
    chip_swap = [
        (i * n_rows + j, partner[i] * n_rows + j if i in partner else i * n_rows + (j ^ 1))
        for i in range(n_frames)
        for j in range(n_rows)
    ]

    def rows_swaps(to_above, to_below):
        first = lax.ppermute(jnp.where(odd, to_above, to_below), "rows", even_swap)
        second = lax.ppermute(jnp.where(odd, to_below, to_above), "rows", odd_swap)
        return first, second

    def swap_core(x):
        return lax.ppermute(x, "frames", core_swap)

    def swap_chip(x):
        return lax.ppermute(x, ("frames", "rows"), chip_swap)

    with jax.named_scope("feature_rows"):
        center = jnp.concatenate([fmap, context], axis=1)
        near_center = swap_chip(center)
        far = lax.ppermute(jnp.where(row < 2, fmap[:, 2:], fmap[:, :1]), "rows", across)
        first, second = rows_swaps(
            jnp.concatenate([fmap, context[:, :1]], axis=1), jnp.concatenate([fmap, context[:, 2:]], axis=1)
        )
        none = jnp.zeros_like(far)
        blank = jnp.zeros_like(first)
        from_above = jnp.where(row > 0, jnp.where(odd, first, second), blank)
        from_below = jnp.where(row < n_rows - 1, jnp.where(odd, second, first), blank)
        halo = jnp.concatenate(
            [
                jnp.where(row < 2, none, far),
                from_above[:, :3],
                from_below[:, :3],
                jnp.where(row < 2, far, none),
                from_above[:, 3:],
                from_below[:, 3:],
            ],
            axis=1,
        )
    halo, pairs = lax.optimization_barrier((halo, pairs))
    idx, flags = slot_table(pairs, index), row_flags(row)
    with jax.named_scope("feature_window"):
        near_halo = swap_chip(halo)
        halo_other = swap_core(halo)
        center_other = swap_core(jnp.concatenate([center, near_center]))
        near_halo_other = swap_core(near_halo)

    with jax.named_scope("first_iteration"):
        sums = [jax.ShapeDtypeStruct((4, OWN, CHANS), BF16)] * 2
        edge_rows = [jax.ShapeDtypeStruct((SLOTS, WIDTH, CHANS), BF16)] * 2
        part, part_other, hid, hid_first, hid_last, motion, base = call(
            first_kernel,
            [
                *sums,
                jax.ShapeDtypeStruct((SLOTS, OWN, CHANS), F32),
                *edge_rows,
                jax.ShapeDtypeStruct((SLOTS, WIDE, CHANS), BF16),
                jax.ShapeDtypeStruct((4, 5, WIDTH, CHANS), BF16),
            ],
            [
                pltpu.VMEM((2, 5, WIDTH, CHANS), BF16),
                pltpu.VMEM((2, 11, WIDTH, CHANS), BF16),
                pltpu.VMEM((2, 5, WIDTH, CHANS), BF16),
                pltpu.VMEM((SLOTS, OWN, CHANS), F32),
                pltpu.VMEM((WIDTH, WIDTH), BF16),
                pltpu.VMEM((CHANS, CHANS), BF16),
                pltpu.VMEM((WIDTH, CHANS), F32),
                pltpu.SMEM((SLOTS,), jnp.int32),
            ],
            2_000_000_000,
            idx, center, near_center, center_other, halo, near_halo, halo_other, near_halo_other, w_corr, w_zr, w_q, w_msg,
        )

    with jax.named_scope("first_sums"):
        mine = part.astype(F32) + swap_core(part_other).astype(F32)
        sent = mine.astype(BF16)
        arrived = swap_chip(sent).astype(F32)
        total = mine + jnp.concatenate([arrived[2:], arrived[:2]])
        upd = jnp.maximum(total, 0.0).astype(BF16).reshape(4, ROWS, WIDTH, CHANS)
    with jax.named_scope("update_rows"):
        first, second = rows_swaps(
            jnp.concatenate([upd[:, :2].reshape(8, WIDTH, CHANS), hid_first]),
            jnp.concatenate([upd[:, 1:].reshape(8, WIDTH, CHANS), hid_last]),
        )
    with jax.named_scope("first_state"):
        [state] = call(
            state_kernel,
            [jax.ShapeDtypeStruct((4, 5, WIDTH, CHANS), BF16)],
            [],
            400_000_000,
            flags, base, upd, first, second, w_res,
        )
        state_other = swap_core(state)
    with jax.named_scope("second_iteration"):
        part, part_other = call(
            second_kernel,
            sums,
            [
                pltpu.VMEM((2, 5, WIDTH, CHANS), BF16),
                pltpu.VMEM((SLOTS, OWN, CHANS), F32),
                pltpu.SMEM((SLOTS,), jnp.int32),
            ],
            1_500_000_000,
            idx, flags, state, state_other, motion, hid, first, second, w_zr, w_q, w_msg,
        )
    with jax.named_scope("second_sums"):
        mine = part.astype(F32) + swap_core(part_other).astype(F32)
        arrived = swap_chip(mine[2:].astype(BF16)).astype(F32)
        upd = jnp.maximum(mine[:2] + arrived, 0.0).astype(BF16).reshape(2, ROWS, WIDTH, CHANS)
        first, second = rows_swaps(upd[:, :1], upd[:, 2:])
    with jax.named_scope("last_state"):
        [out] = call(
            last_kernel,
            [jax.ShapeDtypeStruct((2, ROWS, WIDTH, CHANS), BF16)],
            [],
            120_000_000,
            flags, state, upd, first, second, w_res,
        )
    return out


def solution(mesh):
    placed = (
        P("frames", "rows", None, None),
        P("frames", "rows", None, None),
        P(),
        P(),
        P(),
        P(),
        P(),
        P(),
    )
    return jax.shard_map(
        local,
        mesh=mesh,
        in_specs=placed,
        out_specs=P("frames", "rows", None, None),
        check_vma=False,
    )
```

```python
import jax
import jax.numpy as jnp
from jax import lax
from jax.experimental import pallas as pl
from jax.experimental.pallas import tpu as pltpu
from jax.sharding import PartitionSpec as P

SLOTS = 8
GROUP = 4
ROWS = 3
WIDTH = 64
CHANS = 128
SPAN = 7
WIDE = 5 * WIDTH
OWN = ROWS * WIDTH
F32 = jnp.float32
BF16 = jnp.bfloat16


def dot(a, b):
    return lax.dot_general(a, b, (((1,), (0,)), ((), ())), preferred_element_type=F32)


def dot_t(a, b):
    return lax.dot_general(a, b, (((1,), (1,)), ((), ())), preferred_element_type=F32)


def sigmoid(x):
    return 0.5 * jnp.tanh(0.5 * x) + 0.5


def side_by_side(weights):
    rows = [jnp.concatenate([weights[3 * k + j] for j in range(3)], axis=1) for k in range(3)]
    return jnp.concatenate(rows, axis=0)


def conv_rows(fields, weights, rows):
    size = rows * WIDTH
    taps = [
        jnp.concatenate([field[k * WIDTH : k * WIDTH + size] for k in range(3)], axis=1) for field in fields
    ]
    out = dot(jnp.concatenate(taps), weights)
    size *= len(fields)
    column = lax.broadcasted_iota(jnp.int32, (size, CHANS), 0) & (WIDTH - 1)
    left = jnp.where(column == 0, 0.0, pltpu.roll(out[:, :CHANS], 1, 0))
    right = jnp.where(column == WIDTH - 1, 0.0, pltpu.roll(out[:, 2 * CHANS :], size - 1, 0))
    return out[:, CHANS : 2 * CHANS] + left + right


def gru(hidden, xin, w_zr, w_q):
    joined = [jnp.concatenate([h.astype(BF16), x], axis=1) for h, x in zip(hidden, xin)]
    own = slice(WIDTH, WIDTH + OWN)
    reset = sigmoid(dot(jnp.concatenate(joined), w_zr[:, CHANS:]))
    update = sigmoid(dot(jnp.concatenate([j[own] for j in joined]), w_zr[:, :CHANS]))
    gated = (reset * jnp.concatenate(hidden)).astype(BF16)
    fields = [jnp.concatenate([gated[k * WIDE : (k + 1) * WIDE], x], axis=1) for k, x in enumerate(xin)]
    candidate = jnp.tanh(conv_rows(fields, w_q, ROWS))
    old = jnp.concatenate([h[own] for h in hidden])
    new = old + update * (candidate - old)
    return [new[k * OWN : (k + 1) * OWN] for k in range(len(xin))]


def read_table(table, idx):
    count = 0
    for s in range(SLOTS):
        code = table[0, s]
        idx[s] = code
        count += jnp.where(code >= 0, 1, 0)
    return count


def add_messages(acc, idx, slots, hidden, w_msg):
    messages = dot(jnp.concatenate(hidden).astype(BF16), w_msg)
    for k, s in enumerate(slots):

        @pl.when(idx[s] >= 0)
        def _():
            acc[idx[s] // SLOTS] += messages[k * OWN : (k + 1) * OWN, :CHANS]
            acc[idx[s] % SLOTS] += messages[k * OWN : (k + 1) * OWN, CHANS:]


def give_sums(acc, part, part_other):
    part[...] = acc[:4].astype(BF16)
    part_other[...] = acc[4:].astype(BF16)


def first_kernel(
    table, c0, c1, c23, h0, h1, h2, h3, w_corr, w_zr, w_q, w_msg,
    part, part_other, hid, hid_first, hid_last, motion_out, base,
    feat, rim, ctx, acc, flip, spread, edge, idx,
):
    pieces = ((c0, 0, h0), (c1, 0, h1), (c23, 0, h2), (c23, 2, h3))
    count = read_table(table, idx)
    acc[...] = jnp.zeros_like(acc)
    for half, (center, _, halo) in enumerate(pieces[:2]):
        frames = pl.ds(2 * half, 2)
        base[frames, 0], base[frames, 1:4], base[frames, 4] = halo[:, 8], center[:, 3:6], halo[:, 9]
    ends = [lax.broadcasted_iota(jnp.int32, (WIDTH, WIDTH), k) for k in range(2)]
    flip[...] = jnp.where(ends[0] + ends[1] == WIDTH - 1, 1.0, 0.0).astype(BF16)
    lane, tap = [lax.broadcasted_iota(jnp.int32, (CHANS, SPAN * SPAN), k) for k in range(2)]
    place = (lane & (WIDTH - 1)) - 4
    shift = jnp.where(lane < WIDTH, 2 * (place >> 3), jnp.minimum(2 * (place >> 3) + 1, SPAN - 1))
    wanted = (place >= 0) & (place < 32) & ((place & 7) < SPAN) & (tap == SPAN * shift + (place & 7))
    spread[...] = dot(jnp.where(wanted, 1.0, 0.0).astype(BF16), w_corr[...]).astype(BF16)
    column = WIDTH - 1 - lax.broadcasted_iota(jnp.int32, (WIDTH, CHANS), 0)
    lane = lax.broadcasted_iota(jnp.int32, (WIDTH, CHANS), 1)
    place = (lane & (WIDTH - 1)) - 4
    at = column + (place & 7) - 3
    inside = (place >= 0) & (place < 32) & ((place & 7) < SPAN) & (at >= 0) & (at < WIDTH)
    inside = inside & ((place < 24) | (lane >= WIDTH))
    edge[...] = jnp.where(inside, 1.0 / CHANS**0.5, 0.0)
    place = (lax.broadcasted_iota(jnp.int32, (WIDTH, CHANS), 1) & (WIDTH - 1)) - 4

    def body(i, carry):
        slots = [GROUP * i + j for j in range(GROUP)]
        for j, s in enumerate(slots):
            code = jnp.maximum(idx[s], 0)
            source, target = code // SLOTS, code % SLOTS
            for k, (center, first, halo) in enumerate(pieces):

                @pl.when(source // 2 == k)
                def _():
                    frame = source % 2
                    feat[j, 0], ctx[j, 0] = halo[frame, 3], halo[frame, 8]
                    feat[j, 1:4], ctx[j, 1:4] = center[first + frame, 0:3], center[first + frame, 3:6]
                    feat[j, 4], ctx[j, 4] = halo[frame, 4], halo[frame, 9]

                @pl.when(target // 2 == k)
                def _():
                    frame = target % 2
                    rim[j, 0:4] = halo[frame, 0:4]
                    rim[j, 4:7] = center[first + frame, 0:3]
                    rim[j, 7:11] = halo[frame, 4:8]

        rows = [(j, y) for j in range(GROUP) for y in range(5)]
        turned = dot(flip[...], jnp.concatenate([feat[j, y] for j, y in rows], axis=1)).astype(BF16)
        corr = []
        for j in range(GROUP):
            near = [turned[:, (5 * j + y) * CHANS : (5 * j + y + 1) * CHANS] for y in range(5)]
            totals = [None] * 5
            for t in range(10):
                far = rim[j, t : t + 2].reshape(2 * WIDTH, CHANS)
                uses = [(t - 2 * g, g) for g in range(3) if 0 <= t - 2 * g < 5]
                uses += [(t - 5, 3)] if t >= 5 else []
                table = dot_t(jnp.concatenate([near[y] for y, _ in uses]), far)
                for k, (y, g) in enumerate(uses):
                    part_table = table[k * WIDTH : (k + 1) * WIDTH]
                    moved = pltpu.roll(part_table, 8 * g + 72, 1, stride=1, stride_axis=0)
                    totals[y] = moved if g == 0 else jnp.where(place < 8 * g, totals[y], moved)
            corr += [(total * edge[...]).astype(BF16) for total in totals]
        turned = dot(flip[...], jnp.concatenate(corr, axis=1)).astype(BF16)
        corr = jnp.concatenate([turned[:, k * CHANS : (k + 1) * CHANS] for k in range(len(rows))])
        motion = jnp.maximum(dot(corr, spread[...]), 0.0).astype(BF16)
        motion = [motion[j * WIDE : (j + 1) * WIDE] for j in range(GROUP)]
        state = [ctx[j].reshape(WIDE, CHANS).astype(F32) for j in range(GROUP)]
        xin = [(m.astype(F32) + c).astype(BF16) for m, c in zip(motion, state)]
        hidden = gru([jnp.tanh(c) for c in state], xin, w_zr[...], side_by_side(w_q))
        for s, m, h in zip(slots, motion, hidden):
            motion_out[s] = m
            hid[s] = h
            hid_first[s] = h[:WIDTH].astype(BF16)
            hid_last[s] = h[2 * WIDTH :].astype(BF16)
        add_messages(acc, idx, slots, hidden, w_msg[...])
        return carry

    lax.fori_loop(0, (count + GROUP - 1) // GROUP, body, 0)
    give_sums(acc, part, part_other)


def second_kernel(
    table, flags, s0, s1, motion, hid, first, second, w_zr, w_q, w_msg,
    part, part_other, state_buf, acc, idx,
):
    count = read_table(table, idx)
    acc[...] = jnp.zeros_like(acc)

    def body(i, carry):
        slots = [GROUP * i + j for j in range(GROUP)]
        for j, s in enumerate(slots):
            source = jnp.maximum(idx[s], 0) // SLOTS
            for k, piece in enumerate((s0, s1)):

                @pl.when(source // 4 == k)
                def _():
                    state_buf[j] = piece[source % 4]

        state = [state_buf[j].reshape(WIDE, CHANS).astype(F32) for j in range(GROUP)]
        xin = [(motion[s].astype(F32) + c).astype(BF16) for s, c in zip(slots, state)]
        hidden = []
        for s in slots:
            above, below = arrived(flags, first[SLOTS + s].astype(F32), second[SLOTS + s].astype(F32))
            hidden.append(jnp.concatenate([above, hid[s], below]))
        hidden = gru(hidden, xin, w_zr[...], side_by_side(w_q))
        add_messages(acc, idx, slots, hidden, w_msg[...])
        return carry

    lax.fori_loop(0, (count + GROUP - 1) // GROUP, body, 0)
    give_sums(acc, part, part_other)


def arrived(flags, first, second):
    weight = [flags[k : k + 1].astype(first.dtype) for k in range(4)]
    return first * weight[0] + second * weight[1], first * weight[2] + second * weight[3]


def state_kernel(flags, base, upd, first, second, w_res, out):
    for half in range(2):
        fields = []
        for frame in (2 * half, 2 * half + 1):
            rows = pl.ds(2 * frame, 2)
            above, below = arrived(flags, first[rows].reshape(2 * WIDTH, CHANS), second[rows].reshape(2 * WIDTH, CHANS))
            fields.append(jnp.concatenate([above, upd[frame].reshape(OWN, CHANS), below]))
        new = conv_rows(fields, side_by_side(w_res), 5).reshape(2, 5, WIDTH, CHANS)
        new = (base[2 * half : 2 * half + 2].astype(F32) + new).astype(BF16)
        out[2 * half : 2 * half + 2, 1:4] = new[:, 1:4]
        out[2 * half : 2 * half + 2, 0] = new[:, 0] * flags[4:5].astype(BF16)
        out[2 * half : 2 * half + 2, 4] = new[:, 4] * flags[5:6].astype(BF16)


def last_kernel(flags, state, upd, first, second, w_res, out):
    fields = []
    for frame in range(2):
        above, below = arrived(flags, first[frame, 0], second[frame, 0])
        fields.append(jnp.concatenate([above, upd[frame].reshape(OWN, CHANS), below]))
    new = conv_rows(fields, side_by_side(w_res), ROWS).reshape(2, ROWS, WIDTH, CHANS)
    out[...] = (state[:2, 1:4].astype(F32) + new).astype(BF16)


VM = pl.BlockSpec(memory_space=pltpu.VMEM)


def call(kernel, outs, scratch, flops, *args):
    size = sum(a.size * a.dtype.itemsize for a in args)
    return pl.pallas_call(
        kernel,
        out_shape=outs,
        in_specs=[VM] * len(args),
        out_specs=[VM] * len(outs),
        scratch_shapes=scratch,
        compiler_params=pltpu.CompilerParams(vmem_limit_bytes=14 * 2**20),
        cost_estimate=pl.CostEstimate(flops=flops, bytes_accessed=size, transcendentals=0),
    )(*args)


def slot_table(pairs, index):
    chip, core = index >> 1, index & 1
    sources, targets, owners = (pairs[:, k] for k in range(3))

    def place(frame):
        dev = (frame >> 1) - 2 * chip
        other = jnp.where((dev >= 1) != (core == 1), 4, 0)
        return other + jnp.where((dev < 0) | (dev > 1), 2, 0) + (frame & 1)

    mine = (owners >> 1) == chip
    order = jnp.arange(pairs.shape[0], dtype=jnp.int32)
    ranks = jnp.sum(jnp.where((order[None, :] < order[:, None]) & mine[None, :], 1, 0), axis=1)
    codes = place(sources) * SLOTS + place(targets)
    levels = 2 * jnp.arange(SLOTS, dtype=jnp.int32) + core
    picked = jnp.where((ranks[None, :] == levels[:, None]) & mine[None, :], codes[None, :] + 1, 0)
    picked = jnp.sum(picked, axis=1) - 1
    return picked[None]


def row_flags(row):
    line = lax.broadcasted_iota(jnp.int32, (8, CHANS), 0)
    odd, up, down = row % 2 == 1, row > 0, row < 3
    flags = ((line == 0) & (up & odd)) | ((line == 1) & (up & ~odd)) | ((line == 2) & (down & ~odd))
    flags = flags | ((line == 3) & (down & odd)) | ((line == 4) & up) | ((line == 5) & down)
    return flags.astype(F32)


def local(fmap, context, pairs, w_corr, w_zr, w_q, w_msg, w_res):
    index, row = lax.axis_index("frames"), lax.axis_index("rows")
    n_frames, n_rows = lax.axis_size("frames"), lax.axis_size("rows")
    even_swap = [(i, i ^ 1) for i in range(n_rows)]
    odd_swap = [(i, n_rows - 1 - i) for i in range(n_rows)]
    odd = row % 2 == 1
    across = [(i, (i + 2) % 4) for i in range(n_rows)]
    core_swap = [(i, i ^ 1) for i in range(n_frames)]
    partner = {i: i + 1 if i % 2 else i - 1 for i in range(1, n_frames - 1)}
    chip_swap = [
        (i * n_rows + j, partner[i] * n_rows + j if i in partner else i * n_rows + (j ^ 1))
        for i in range(n_frames)
        for j in range(n_rows)
    ]

    def rows_swaps(to_above, to_below):
        first = lax.ppermute(jnp.where(odd, to_above, to_below), "rows", even_swap)
        second = lax.ppermute(jnp.where(odd, to_below, to_above), "rows", odd_swap)
        return first, second

    def swap_core(x):
        return lax.ppermute(x, "frames", core_swap)

    def swap_chip(x):
        return lax.ppermute(x, ("frames", "rows"), chip_swap)

    with jax.named_scope("feature_rows"):
        center = jnp.concatenate([fmap, context], axis=1)
        near_center = swap_chip(center)
        far = lax.ppermute(jnp.where(row < 2, fmap[:, 2:], fmap[:, :1]), "rows", across)
        first, second = rows_swaps(
            jnp.concatenate([fmap, context[:, :1]], axis=1), jnp.concatenate([fmap, context[:, 2:]], axis=1)
        )
        none = jnp.zeros_like(far)
        blank = jnp.zeros_like(first)
        from_above = jnp.where(row > 0, jnp.where(odd, first, second), blank)
        from_below = jnp.where(row < n_rows - 1, jnp.where(odd, second, first), blank)
        halo = jnp.concatenate(
            [
                jnp.where(row < 2, none, far),
                from_above[:, :3],
                from_below[:, :3],
                jnp.where(row < 2, far, none),
                from_above[:, 3:],
                from_below[:, 3:],
            ],
            axis=1,
        )
    halo, pairs = lax.optimization_barrier((halo, pairs))
    idx, flags = slot_table(pairs, index), row_flags(row)
    with jax.named_scope("feature_window"):
        near_halo = swap_chip(halo)
        halo_other = swap_core(halo)
        center_other = swap_core(jnp.concatenate([center, near_center]))
        near_halo_other = swap_core(near_halo)

    with jax.named_scope("first_iteration"):
        sums = [jax.ShapeDtypeStruct((4, OWN, CHANS), BF16)] * 2
        edge_rows = [jax.ShapeDtypeStruct((SLOTS, WIDTH, CHANS), BF16)] * 2
        part, part_other, hid, hid_first, hid_last, motion, base = call(
            first_kernel,
            [
                *sums,
                jax.ShapeDtypeStruct((SLOTS, OWN, CHANS), F32),
                *edge_rows,
                jax.ShapeDtypeStruct((SLOTS, WIDE, CHANS), BF16),
                jax.ShapeDtypeStruct((4, 5, WIDTH, CHANS), BF16),
            ],
            [
                pltpu.VMEM((GROUP, 5, WIDTH, CHANS), BF16),
                pltpu.VMEM((GROUP, 11, WIDTH, CHANS), BF16),
                pltpu.VMEM((GROUP, 5, WIDTH, CHANS), BF16),
                pltpu.VMEM((SLOTS, OWN, CHANS), F32),
                pltpu.VMEM((WIDTH, WIDTH), BF16),
                pltpu.VMEM((CHANS, CHANS), BF16),
                pltpu.VMEM((WIDTH, CHANS), F32),
                pltpu.SMEM((SLOTS,), jnp.int32),
            ],
            2_000_000_000,
            idx, center, near_center, center_other, halo, near_halo, halo_other, near_halo_other, w_corr, w_zr, w_q, w_msg,
        )

    with jax.named_scope("first_sums"):
        mine = part.astype(F32) + swap_core(part_other).astype(F32)
        sent = mine.astype(BF16)
        arrived = swap_chip(sent).astype(F32)
        total = mine + jnp.concatenate([arrived[2:], arrived[:2]])
        upd = jnp.maximum(total, 0.0).astype(BF16).reshape(4, ROWS, WIDTH, CHANS)
    with jax.named_scope("update_rows"):
        first, second = rows_swaps(
            jnp.concatenate([upd[:, :2].reshape(8, WIDTH, CHANS), hid_first]),
            jnp.concatenate([upd[:, 1:].reshape(8, WIDTH, CHANS), hid_last]),
        )
    with jax.named_scope("first_state"):
        [state] = call(
            state_kernel,
            [jax.ShapeDtypeStruct((4, 5, WIDTH, CHANS), BF16)],
            [],
            400_000_000,
            flags, base, upd, first, second, w_res,
        )
        state_other = swap_core(state)
    with jax.named_scope("second_iteration"):
        part, part_other = call(
            second_kernel,
            sums,
            [
                pltpu.VMEM((GROUP, 5, WIDTH, CHANS), BF16),
                pltpu.VMEM((SLOTS, OWN, CHANS), F32),
                pltpu.SMEM((SLOTS,), jnp.int32),
            ],
            1_500_000_000,
            idx, flags, state, state_other, motion, hid, first, second, w_zr, w_q, w_msg,
        )
    with jax.named_scope("second_sums"):
        mine = part.astype(F32) + swap_core(part_other).astype(F32)
        arrived = swap_chip(mine[2:].astype(BF16)).astype(F32)
        upd = jnp.maximum(mine[:2] + arrived, 0.0).astype(BF16).reshape(2, ROWS, WIDTH, CHANS)
        first, second = rows_swaps(upd[:, :1], upd[:, 2:])
    with jax.named_scope("last_state"):
        [out] = call(
            last_kernel,
            [jax.ShapeDtypeStruct((2, ROWS, WIDTH, CHANS), BF16)],
            [],
            120_000_000,
            flags, state, upd, first, second, w_res,
        )
    return out


def solution(mesh):
    placed = (
        P("frames", "rows", None, None),
        P("frames", "rows", None, None),
        P(),
        P(),
        P(),
        P(),
        P(),
        P(),
    )
    return jax.shard_map(
        local,
        mesh=mesh,
        in_specs=placed,
        out_specs=P("frames", "rows", None, None),
        check_vma=False,
    )
```

```python
import jax
import jax.numpy as jnp
from jax import lax
from jax.experimental import pallas as pl
from jax.experimental.pallas import tpu as pltpu
from jax.sharding import PartitionSpec as P

SLOTS = 8
GROUP = 4
ROWS = 3
WIDTH = 64
CHANS = 128
SPAN = 7
WIDE = 5 * WIDTH
OWN = ROWS * WIDTH
F32 = jnp.float32
BF16 = jnp.bfloat16


def dot(a, b):
    return lax.dot_general(a, b, (((1,), (0,)), ((), ())), preferred_element_type=F32)


def dot_t(a, b):
    return lax.dot_general(a, b, (((1,), (1,)), ((), ())), preferred_element_type=F32)


def sigmoid(x):
    return 0.5 * jnp.tanh(0.5 * x) + 0.5


def side_by_side(weights):
    rows = [jnp.concatenate([weights[3 * k + j] for j in range(3)], axis=1) for k in range(3)]
    return jnp.concatenate(rows, axis=0)


def conv_rows(fields, weights, rows):
    size = rows * WIDTH
    taps = [
        jnp.concatenate([field[k * WIDTH : k * WIDTH + size] for k in range(3)], axis=1) for field in fields
    ]
    out = dot(jnp.concatenate(taps), weights)
    size *= len(fields)
    column = lax.broadcasted_iota(jnp.int32, (size, CHANS), 0) & (WIDTH - 1)
    left = jnp.where(column == 0, 0.0, pltpu.roll(out[:, :CHANS], 1, 0))
    right = jnp.where(column == WIDTH - 1, 0.0, pltpu.roll(out[:, 2 * CHANS :], size - 1, 0))
    return out[:, CHANS : 2 * CHANS] + left + right


def gru(hidden, xin, w_zr, w_q):
    joined = [jnp.concatenate([h.astype(BF16), x], axis=1) for h, x in zip(hidden, xin)]
    own = slice(WIDTH, WIDTH + OWN)
    reset = sigmoid(dot(jnp.concatenate(joined), w_zr[:, CHANS:]))
    update = sigmoid(dot(jnp.concatenate([j[own] for j in joined]), w_zr[:, :CHANS]))
    gated = (reset * jnp.concatenate(hidden)).astype(BF16)
    fields = [jnp.concatenate([gated[k * WIDE : (k + 1) * WIDE], x], axis=1) for k, x in enumerate(xin)]
    candidate = jnp.tanh(conv_rows(fields, w_q, ROWS))
    old = jnp.concatenate([h[own] for h in hidden])
    new = old + update * (candidate - old)
    return [new[k * OWN : (k + 1) * OWN] for k in range(len(xin))]


def read_table(table, idx):
    count = 0
    for s in range(SLOTS):
        code = table[0, s]
        idx[s] = code
        count += jnp.where(code >= 0, 1, 0)
    return count


def add_messages(acc, idx, slots, hidden, w_msg):
    messages = dot(jnp.concatenate(hidden).astype(BF16), w_msg)
    for k, s in enumerate(slots):

        @pl.when(idx[s] >= 0)
        def _():
            acc[idx[s] // SLOTS] += messages[k * OWN : (k + 1) * OWN, :CHANS]
            acc[idx[s] % SLOTS] += messages[k * OWN : (k + 1) * OWN, CHANS:]


def give_sums(acc, part, part_other):
    part[...] = acc[:4].astype(BF16)
    part_other[...] = acc[4:].astype(BF16)


def tables_kernel(w_corr, flip, spread, edge):
    ends = [lax.broadcasted_iota(jnp.int32, (WIDTH, WIDTH), k) for k in range(2)]
    flip[...] = jnp.where(ends[0] + ends[1] == WIDTH - 1, 1.0, 0.0).astype(BF16)
    lane, tap = [lax.broadcasted_iota(jnp.int32, (CHANS, SPAN * SPAN), k) for k in range(2)]
    place = (lane & (WIDTH - 1)) - 4
    shift = jnp.where(lane < WIDTH, 2 * (place >> 3), jnp.minimum(2 * (place >> 3) + 1, SPAN - 1))
    wanted = (place >= 0) & (place < 32) & ((place & 7) < SPAN) & (tap == SPAN * shift + (place & 7))
    spread[...] = dot(jnp.where(wanted, 1.0, 0.0).astype(BF16), w_corr[...]).astype(BF16)
    column = WIDTH - 1 - lax.broadcasted_iota(jnp.int32, (WIDTH, CHANS), 0)
    lane = lax.broadcasted_iota(jnp.int32, (WIDTH, CHANS), 1)
    place = (lane & (WIDTH - 1)) - 4
    at = column + (place & 7) - 3
    inside = (place >= 0) & (place < 32) & ((place & 7) < SPAN) & (at >= 0) & (at < WIDTH)
    inside = inside & ((place < 24) | (lane >= WIDTH))
    edge[...] = jnp.where(inside, 1.0 / CHANS**0.5, 0.0)


def first_kernel(
    table, c0, c1, c23, h0, h1, h2, h3, flip, spread, edge, w_zr, w_q, w_msg,
    part, part_other, hid, hid_first, hid_last, motion_out, base,
    feat, rim, ctx, acc, idx,
):
    pieces = ((c0, 0, h0), (c1, 0, h1), (c23, 0, h2), (c23, 2, h3))
    count = read_table(table, idx)
    acc[...] = jnp.zeros_like(acc)
    for half, (center, _, halo) in enumerate(pieces[:2]):
        frames = pl.ds(2 * half, 2)
        base[frames, 0], base[frames, 1:4], base[frames, 4] = halo[:, 8], center[:, 3:6], halo[:, 9]
    place = (lax.broadcasted_iota(jnp.int32, (WIDTH, CHANS), 1) & (WIDTH - 1)) - 4

    def body(i, carry):
        slots = [GROUP * i + j for j in range(GROUP)]
        for j, s in enumerate(slots):
            code = jnp.maximum(idx[s], 0)
            source, target = code // SLOTS, code % SLOTS
            for k, (center, first, halo) in enumerate(pieces):

                @pl.when(source // 2 == k)
                def _():
                    frame = source % 2
                    feat[j, 0], ctx[j, 0] = halo[frame, 3], halo[frame, 8]
                    feat[j, 1:4], ctx[j, 1:4] = center[first + frame, 0:3], center[first + frame, 3:6]
                    feat[j, 4], ctx[j, 4] = halo[frame, 4], halo[frame, 9]

                @pl.when(target // 2 == k)
                def _():
                    frame = target % 2
                    rim[j, 0:4] = halo[frame, 0:4]
                    rim[j, 4:7] = center[first + frame, 0:3]
                    rim[j, 7:11] = halo[frame, 4:8]

        rows = [(j, y) for j in range(GROUP) for y in range(5)]
        turned = dot(flip[...], jnp.concatenate([feat[j, y] for j, y in rows], axis=1)).astype(BF16)
        corr = []
        for j in range(GROUP):
            near = [turned[:, (5 * j + y) * CHANS : (5 * j + y + 1) * CHANS] for y in range(5)]
            totals = [None] * 5
            for t in range(10):
                far = rim[j, t : t + 2].reshape(2 * WIDTH, CHANS)
                uses = [(t - 2 * g, g) for g in range(3) if 0 <= t - 2 * g < 5]
                uses += [(t - 5, 3)] if t >= 5 else []
                table = dot_t(jnp.concatenate([near[y] for y, _ in uses]), far)
                for k, (y, g) in enumerate(uses):
                    part_table = table[k * WIDTH : (k + 1) * WIDTH]
                    moved = pltpu.roll(part_table, 8 * g + 72, 1, stride=1, stride_axis=0)
                    totals[y] = moved if g == 0 else jnp.where(place < 8 * g, totals[y], moved)
            corr += [(total * edge[...]).astype(BF16) for total in totals]
        turned = dot(flip[...], jnp.concatenate(corr, axis=1)).astype(BF16)
        corr = jnp.concatenate([turned[:, k * CHANS : (k + 1) * CHANS] for k in range(len(rows))])
        motion = jnp.maximum(dot(corr, spread[...]), 0.0).astype(BF16)
        motion = [motion[j * WIDE : (j + 1) * WIDE] for j in range(GROUP)]
        state = [ctx[j].reshape(WIDE, CHANS).astype(F32) for j in range(GROUP)]
        xin = [(m.astype(F32) + c).astype(BF16) for m, c in zip(motion, state)]
        hidden = gru([jnp.tanh(c) for c in state], xin, w_zr[...], side_by_side(w_q))
        for s, m, h in zip(slots, motion, hidden):
            motion_out[s] = m
            hid[s] = h
            hid_first[s] = h[:WIDTH].astype(BF16)
            hid_last[s] = h[2 * WIDTH :].astype(BF16)
        add_messages(acc, idx, slots, hidden, w_msg[...])
        return carry

    lax.fori_loop(0, (count + GROUP - 1) // GROUP, body, 0)
    give_sums(acc, part, part_other)


def second_kernel(
    table, flags, s0, s1, motion, hid, first, second, w_zr, w_q, w_msg,
    part, part_other, state_buf, acc, idx,
):
    count = read_table(table, idx)
    acc[...] = jnp.zeros_like(acc)

    def body(i, carry):
        slots = [GROUP * i + j for j in range(GROUP)]
        for j, s in enumerate(slots):
            source = jnp.maximum(idx[s], 0) // SLOTS
            for k, piece in enumerate((s0, s1)):

                @pl.when(source // 4 == k)
                def _():
                    state_buf[j] = piece[source % 4]

        state = [state_buf[j].reshape(WIDE, CHANS).astype(F32) for j in range(GROUP)]
        xin = [(motion[s].astype(F32) + c).astype(BF16) for s, c in zip(slots, state)]
        hidden = []
        for s in slots:
            above, below = arrived(flags, first[SLOTS + s].astype(F32), second[SLOTS + s].astype(F32))
            hidden.append(jnp.concatenate([above, hid[s], below]))
        hidden = gru(hidden, xin, w_zr[...], side_by_side(w_q))
        add_messages(acc, idx, slots, hidden, w_msg[...])
        return carry

    lax.fori_loop(0, (count + GROUP - 1) // GROUP, body, 0)
    give_sums(acc, part, part_other)


def arrived(flags, first, second):
    weight = [flags[k : k + 1].astype(first.dtype) for k in range(4)]
    return first * weight[0] + second * weight[1], first * weight[2] + second * weight[3]


def state_kernel(flags, base, upd, first, second, w_res, out):
    for half in range(2):
        fields = []
        for frame in (2 * half, 2 * half + 1):
            rows = pl.ds(2 * frame, 2)
            above, below = arrived(flags, first[rows].reshape(2 * WIDTH, CHANS), second[rows].reshape(2 * WIDTH, CHANS))
            fields.append(jnp.concatenate([above, upd[frame].reshape(OWN, CHANS), below]))
        new = conv_rows(fields, side_by_side(w_res), 5).reshape(2, 5, WIDTH, CHANS)
        new = (base[2 * half : 2 * half + 2].astype(F32) + new).astype(BF16)
        out[2 * half : 2 * half + 2, 1:4] = new[:, 1:4]
        out[2 * half : 2 * half + 2, 0] = new[:, 0] * flags[4:5].astype(BF16)
        out[2 * half : 2 * half + 2, 4] = new[:, 4] * flags[5:6].astype(BF16)


def last_kernel(flags, state, upd, first, second, w_res, out):
    fields = []
    for frame in range(2):
        above, below = arrived(flags, first[frame, 0], second[frame, 0])
        fields.append(jnp.concatenate([above, upd[frame].reshape(OWN, CHANS), below]))
    new = conv_rows(fields, side_by_side(w_res), ROWS).reshape(2, ROWS, WIDTH, CHANS)
    out[...] = (state[:2, 1:4].astype(F32) + new).astype(BF16)


VM = pl.BlockSpec(memory_space=pltpu.VMEM)


def call(kernel, outs, scratch, flops, *args):
    size = sum(a.size * a.dtype.itemsize for a in args)
    return pl.pallas_call(
        kernel,
        out_shape=outs,
        in_specs=[VM] * len(args),
        out_specs=[VM] * len(outs),
        scratch_shapes=scratch,
        compiler_params=pltpu.CompilerParams(vmem_limit_bytes=14 * 2**20),
        cost_estimate=pl.CostEstimate(flops=flops, bytes_accessed=size, transcendentals=0),
    )(*args)


def slot_table(pairs, index):
    chip, core = index >> 1, index & 1
    sources, targets, owners = (pairs[:, k] for k in range(3))

    def place(frame):
        dev = (frame >> 1) - 2 * chip
        other = jnp.where((dev >= 1) != (core == 1), 4, 0)
        return other + jnp.where((dev < 0) | (dev > 1), 2, 0) + (frame & 1)

    mine = (owners >> 1) == chip
    order = jnp.arange(pairs.shape[0], dtype=jnp.int32)
    ranks = jnp.sum(jnp.where((order[None, :] < order[:, None]) & mine[None, :], 1, 0), axis=1)
    codes = place(sources) * SLOTS + place(targets)
    levels = 2 * jnp.arange(SLOTS, dtype=jnp.int32) + core
    picked = jnp.where((ranks[None, :] == levels[:, None]) & mine[None, :], codes[None, :] + 1, 0)
    picked = jnp.sum(picked, axis=1) - 1
    return picked[None]


def row_flags(row):
    line = lax.broadcasted_iota(jnp.int32, (8, CHANS), 0)
    odd, up, down = row % 2 == 1, row > 0, row < 3
    flags = ((line == 0) & (up & odd)) | ((line == 1) & (up & ~odd)) | ((line == 2) & (down & ~odd))
    flags = flags | ((line == 3) & (down & odd)) | ((line == 4) & up) | ((line == 5) & down)
    return flags.astype(F32)


def local(fmap, context, pairs, w_corr, w_zr, w_q, w_msg, w_res):
    index, row = lax.axis_index("frames"), lax.axis_index("rows")
    n_frames, n_rows = lax.axis_size("frames"), lax.axis_size("rows")
    even_swap = [(i, i ^ 1) for i in range(n_rows)]
    odd_swap = [(i, n_rows - 1 - i) for i in range(n_rows)]
    odd = row % 2 == 1
    across = [(i, (i + 2) % 4) for i in range(n_rows)]
    core_swap = [(i, i ^ 1) for i in range(n_frames)]
    partner = {i: i + 1 if i % 2 else i - 1 for i in range(1, n_frames - 1)}
    chip_swap = [
        (i * n_rows + j, partner[i] * n_rows + j if i in partner else i * n_rows + (j ^ 1))
        for i in range(n_frames)
        for j in range(n_rows)
    ]

    def rows_swaps(to_above, to_below):
        first = lax.ppermute(jnp.where(odd, to_above, to_below), "rows", even_swap)
        second = lax.ppermute(jnp.where(odd, to_below, to_above), "rows", odd_swap)
        return first, second

    def swap_core(x):
        return lax.ppermute(x, "frames", core_swap)

    def swap_chip(x):
        return lax.ppermute(x, ("frames", "rows"), chip_swap)

    with jax.named_scope("feature_rows"):
        center = jnp.concatenate([fmap, context], axis=1)
        near_center = swap_chip(center)
        far = lax.ppermute(jnp.where(row < 2, fmap[:, 2:], fmap[:, :1]), "rows", across)
        first, second = rows_swaps(
            jnp.concatenate([fmap, context[:, :1]], axis=1), jnp.concatenate([fmap, context[:, 2:]], axis=1)
        )
        none = jnp.zeros_like(far)
        blank = jnp.zeros_like(first)
        from_above = jnp.where(row > 0, jnp.where(odd, first, second), blank)
        from_below = jnp.where(row < n_rows - 1, jnp.where(odd, second, first), blank)
        halo = jnp.concatenate(
            [
                jnp.where(row < 2, none, far),
                from_above[:, :3],
                from_below[:, :3],
                jnp.where(row < 2, far, none),
                from_above[:, 3:],
                from_below[:, 3:],
            ],
            axis=1,
        )
    halo, pairs, w_corr = lax.optimization_barrier((halo, pairs, w_corr))
    idx, flags = slot_table(pairs, index), row_flags(row)
    tables = call(
        tables_kernel,
        [
            jax.ShapeDtypeStruct((WIDTH, WIDTH), BF16),
            jax.ShapeDtypeStruct((CHANS, CHANS), BF16),
            jax.ShapeDtypeStruct((WIDTH, CHANS), F32),
        ],
        [],
        2_000_000,
        w_corr,
    )
    with jax.named_scope("feature_window"):
        near_halo = swap_chip(halo)
        halo_other = swap_core(halo)
        center_other = swap_core(jnp.concatenate([center, near_center]))
        near_halo_other = swap_core(near_halo)

    with jax.named_scope("first_iteration"):
        sums = [jax.ShapeDtypeStruct((4, OWN, CHANS), BF16)] * 2
        edge_rows = [jax.ShapeDtypeStruct((SLOTS, WIDTH, CHANS), BF16)] * 2
        part, part_other, hid, hid_first, hid_last, motion, base = call(
            first_kernel,
            [
                *sums,
                jax.ShapeDtypeStruct((SLOTS, OWN, CHANS), F32),
                *edge_rows,
                jax.ShapeDtypeStruct((SLOTS, WIDE, CHANS), BF16),
                jax.ShapeDtypeStruct((4, 5, WIDTH, CHANS), BF16),
            ],
            [
                pltpu.VMEM((GROUP, 5, WIDTH, CHANS), BF16),
                pltpu.VMEM((GROUP, 11, WIDTH, CHANS), BF16),
                pltpu.VMEM((GROUP, 5, WIDTH, CHANS), BF16),
                pltpu.VMEM((SLOTS, OWN, CHANS), F32),
                pltpu.SMEM((SLOTS,), jnp.int32),
            ],
            2_000_000_000,
            idx, center, near_center, center_other, halo, near_halo, halo_other, near_halo_other, *tables, w_zr, w_q, w_msg,
        )

    with jax.named_scope("first_sums"):
        mine = part.astype(F32) + swap_core(part_other).astype(F32)
        sent = mine.astype(BF16)
        arrived = swap_chip(sent).astype(F32)
        total = mine + jnp.concatenate([arrived[2:], arrived[:2]])
        upd = jnp.maximum(total, 0.0).astype(BF16).reshape(4, ROWS, WIDTH, CHANS)
    with jax.named_scope("update_rows"):
        first, second = rows_swaps(
            jnp.concatenate([upd[:, :2].reshape(8, WIDTH, CHANS), hid_first]),
            jnp.concatenate([upd[:, 1:].reshape(8, WIDTH, CHANS), hid_last]),
        )
    with jax.named_scope("first_state"):
        [state] = call(
            state_kernel,
            [jax.ShapeDtypeStruct((4, 5, WIDTH, CHANS), BF16)],
            [],
            400_000_000,
            flags, base, upd, first, second, w_res,
        )
        state_other = swap_core(state)
    with jax.named_scope("second_iteration"):
        part, part_other = call(
            second_kernel,
            sums,
            [
                pltpu.VMEM((GROUP, 5, WIDTH, CHANS), BF16),
                pltpu.VMEM((SLOTS, OWN, CHANS), F32),
                pltpu.SMEM((SLOTS,), jnp.int32),
            ],
            1_500_000_000,
            idx, flags, state, state_other, motion, hid, first, second, w_zr, w_q, w_msg,
        )
    with jax.named_scope("second_sums"):
        mine = part.astype(F32) + swap_core(part_other).astype(F32)
        arrived = swap_chip(mine[2:].astype(BF16)).astype(F32)
        upd = jnp.maximum(mine[:2] + arrived, 0.0).astype(BF16).reshape(2, ROWS, WIDTH, CHANS)
        first, second = rows_swaps(upd[:, :1], upd[:, 2:])
    with jax.named_scope("last_state"):
        [out] = call(
            last_kernel,
            [jax.ShapeDtypeStruct((2, ROWS, WIDTH, CHANS), BF16)],
            [],
            120_000_000,
            flags, state, upd, first, second, w_res,
        )
    return out


def solution(mesh):
    placed = (
        P("frames", "rows", None, None),
        P("frames", "rows", None, None),
        P(),
        P(),
        P(),
        P(),
        P(),
        P(),
    )
    return jax.shard_map(
        local,
        mesh=mesh,
        in_specs=placed,
        out_specs=P("frames", "rows", None, None),
        check_vma=False,
    )
```

```python
import jax
import jax.numpy as jnp
from jax import lax
from jax.experimental import pallas as pl
from jax.experimental.pallas import tpu as pltpu
from jax.sharding import PartitionSpec as P

SLOTS = 8
GROUP = 4
ROWS = 3
WIDTH = 64
CHANS = 128
SPAN = 7
WIDE = 5 * WIDTH
OWN = ROWS * WIDTH
F32 = jnp.float32
BF16 = jnp.bfloat16


def dot(a, b):
    return lax.dot_general(a, b, (((1,), (0,)), ((), ())), preferred_element_type=F32)


def dot_t(a, b):
    return lax.dot_general(a, b, (((1,), (1,)), ((), ())), preferred_element_type=F32)


def sigmoid(x):
    return 0.5 * jnp.tanh(0.5 * x) + 0.5


def side_by_side(weights):
    rows = [jnp.concatenate([weights[3 * k + j] for j in range(3)], axis=1) for k in range(3)]
    return jnp.concatenate(rows, axis=0)


def conv_rows(fields, weights, rows):
    size = rows * WIDTH
    taps = [
        jnp.concatenate([field[k * WIDTH : k * WIDTH + size] for k in range(3)], axis=1) for field in fields
    ]
    out = dot(jnp.concatenate(taps), weights)
    size *= len(fields)
    column = lax.broadcasted_iota(jnp.int32, (size, CHANS), 0) & (WIDTH - 1)
    left = jnp.where(column == 0, 0.0, pltpu.roll(out[:, :CHANS], 1, 0))
    right = jnp.where(column == WIDTH - 1, 0.0, pltpu.roll(out[:, 2 * CHANS :], size - 1, 0))
    return out[:, CHANS : 2 * CHANS] + left + right


def gru(hidden, xin, w_zr, w_q):
    joined = [jnp.concatenate([h.astype(BF16), x], axis=1) for h, x in zip(hidden, xin)]
    own = slice(WIDTH, WIDTH + OWN)
    reset = sigmoid(dot(jnp.concatenate(joined), w_zr[:, CHANS:]))
    update = sigmoid(dot(jnp.concatenate([j[own] for j in joined]), w_zr[:, :CHANS]))
    gated = (reset * jnp.concatenate(hidden)).astype(BF16)
    fields = [jnp.concatenate([gated[k * WIDE : (k + 1) * WIDE], x], axis=1) for k, x in enumerate(xin)]
    candidate = jnp.tanh(conv_rows(fields, w_q, ROWS))
    old = jnp.concatenate([h[own] for h in hidden])
    new = old + update * (candidate - old)
    return [new[k * OWN : (k + 1) * OWN] for k in range(len(xin))]


def read_table(table, idx):
    count = 0
    for s in range(SLOTS):
        code = table[0, s]
        idx[s] = code
        count += jnp.where(code >= 0, 1, 0)
    return count


def add_messages(acc, idx, slots, hidden, w_msg):
    messages = dot(jnp.concatenate(hidden).astype(BF16), w_msg)
    for k, s in enumerate(slots):

        @pl.when(idx[s] >= 0)
        def _():
            acc[idx[s] // SLOTS] += messages[k * OWN : (k + 1) * OWN, :CHANS]
            acc[idx[s] % SLOTS] += messages[k * OWN : (k + 1) * OWN, CHANS:]


def give_sums(acc, part, part_other):
    part[...] = acc[:4].astype(BF16)
    part_other[...] = acc[4:].astype(BF16)


def tables_kernel(w_corr, flip, spread, edge):
    ends = [lax.broadcasted_iota(jnp.int32, (WIDTH, WIDTH), k) for k in range(2)]
    flip[...] = jnp.where(ends[0] + ends[1] == WIDTH - 1, 1.0, 0.0).astype(BF16)
    lane, tap = [lax.broadcasted_iota(jnp.int32, (CHANS, SPAN * SPAN), k) for k in range(2)]
    place = (lane & (WIDTH - 1)) - 4
    shift = jnp.where(lane < WIDTH, 2 * (place >> 3), jnp.minimum(2 * (place >> 3) + 1, SPAN - 1))
    wanted = (place >= 0) & (place < 32) & ((place & 7) < SPAN) & (tap == SPAN * shift + (place & 7))
    spread[...] = dot(jnp.where(wanted, 1.0, 0.0).astype(BF16), w_corr[...]).astype(BF16)
    column = WIDTH - 1 - lax.broadcasted_iota(jnp.int32, (WIDTH, CHANS), 0)
    lane = lax.broadcasted_iota(jnp.int32, (WIDTH, CHANS), 1)
    place = (lane & (WIDTH - 1)) - 4
    at = column + (place & 7) - 3
    inside = (place >= 0) & (place < 32) & ((place & 7) < SPAN) & (at >= 0) & (at < WIDTH)
    inside = inside & ((place < 24) | (lane >= WIDTH))
    edge[...] = jnp.where(inside, 1.0 / CHANS**0.5, 0.0)


def first_kernel(
    table, c0, c1, c23, h0, h1, h2, h3, flip, spread, edge, w_zr, w_q, w_msg,
    part, part_other, hid, hid_first, hid_last, motion_out, base,
    feat, rim, ctx, acc, idx,
):
    pieces = ((c0, 0, h0), (c1, 0, h1), (c23, 0, h2), (c23, 2, h3))
    count = read_table(table, idx)
    acc[...] = jnp.zeros_like(acc)
    for half, (center, _, halo) in enumerate(pieces[:2]):
        frames = pl.ds(2 * half, 2)
        base[frames, 0], base[frames, 1:4], base[frames, 4] = halo[:, 8], center[:, 3:6], halo[:, 9]
    place = (lax.broadcasted_iota(jnp.int32, (WIDTH, CHANS), 1) & (WIDTH - 1)) - 4

    def body(i, carry):
        slots = [GROUP * i + j for j in range(GROUP)]
        for j, s in enumerate(slots):
            code = jnp.maximum(idx[s], 0)
            source, target = code // SLOTS, code % SLOTS
            for k, (center, first, halo) in enumerate(pieces):

                @pl.when(source // 2 == k)
                def _():
                    frame = source % 2
                    feat[j, 0], ctx[j, 0] = halo[frame, 3], halo[frame, 8]
                    feat[j, 1:4], ctx[j, 1:4] = center[first + frame, 0:3], center[first + frame, 3:6]
                    feat[j, 4], ctx[j, 4] = halo[frame, 4], halo[frame, 9]

                @pl.when(target // 2 == k)
                def _():
                    frame = target % 2
                    rim[j, 0:4] = halo[frame, 0:4]
                    rim[j, 4:7] = center[first + frame, 0:3]
                    rim[j, 7:11] = halo[frame, 4:8]

        rows = [(j, y) for j in range(GROUP) for y in range(5)]
        turned = dot(flip[...], jnp.concatenate([feat[j, y] for j, y in rows], axis=1)).astype(BF16)
        corr = []
        for j in range(GROUP):
            near = [turned[:, (5 * j + y) * CHANS : (5 * j + y + 1) * CHANS] for y in range(5)]
            totals = [None] * 5
            for t in range(10):
                far = rim[j, t : t + 2].reshape(2 * WIDTH, CHANS)
                uses = [(t - 2 * g, g) for g in range(3) if 0 <= t - 2 * g < 5]
                uses += [(t - 5, 3)] if t >= 5 else []
                table = dot_t(jnp.concatenate([near[y] for y, _ in uses]), far)
                for k, (y, g) in enumerate(uses):
                    part_table = table[k * WIDTH : (k + 1) * WIDTH]
                    moved = pltpu.roll(part_table, 8 * g + 72, 1, stride=1, stride_axis=0)
                    totals[y] = moved if g == 0 else jnp.where(place < 8 * g, totals[y], moved)
            corr += [(total * edge[...]).astype(BF16) for total in totals]
        turned = dot(flip[...], jnp.concatenate(corr, axis=1)).astype(BF16)
        corr = jnp.concatenate([turned[:, k * CHANS : (k + 1) * CHANS] for k in range(len(rows))])
        motion = jnp.maximum(dot(corr, spread[...]), 0.0).astype(BF16)
        motion = [motion[j * WIDE : (j + 1) * WIDE] for j in range(GROUP)]
        state = [ctx[j].reshape(WIDE, CHANS).astype(F32) for j in range(GROUP)]
        xin = [(m.astype(F32) + c).astype(BF16) for m, c in zip(motion, state)]
        hidden = gru([jnp.tanh(c) for c in state], xin, w_zr[...], side_by_side(w_q))
        for s, m, h in zip(slots, motion, hidden):
            motion_out[s] = m
            hid[s] = h
            hid_first[s] = h[:WIDTH].astype(BF16)
            hid_last[s] = h[2 * WIDTH :].astype(BF16)
        add_messages(acc, idx, slots, hidden, w_msg[...])
        return carry

    lax.fori_loop(0, (count + GROUP - 1) // GROUP, body, 0)
    give_sums(acc, part, part_other)


def second_kernel(
    table, flags, s0, s1, motion, hid, first, second, w_zr, w_q, w_msg,
    part, part_other, state_buf, acc, idx,
):
    count = read_table(table, idx)
    acc[...] = jnp.zeros_like(acc)

    def body(i, carry):
        slots = [GROUP * i + j for j in range(GROUP)]
        for j, s in enumerate(slots):
            source = jnp.maximum(idx[s], 0) // SLOTS
            for k, piece in enumerate((s0, s1)):

                @pl.when(source // 4 == k)
                def _():
                    state_buf[j] = piece[source % 4]

        state = [state_buf[j].reshape(WIDE, CHANS).astype(F32) for j in range(GROUP)]
        xin = [(motion[s].astype(F32) + c).astype(BF16) for s, c in zip(slots, state)]
        hidden = []
        for s in slots:
            above, below = arrived(flags, first[SLOTS + s].astype(F32), second[SLOTS + s].astype(F32))
            hidden.append(jnp.concatenate([above, hid[s], below]))
        hidden = gru(hidden, xin, w_zr[...], side_by_side(w_q))
        add_messages(acc, idx, slots, hidden, w_msg[...])
        return carry

    lax.fori_loop(0, (count + GROUP - 1) // GROUP, body, 0)
    give_sums(acc, part, part_other)


def arrived(flags, first, second):
    weight = [flags[k : k + 1].astype(first.dtype) for k in range(4)]
    return first * weight[0] + second * weight[1], first * weight[2] + second * weight[3]


def state_kernel(flags, base, upd, first, second, w_res, out):
    fields = []
    for frame in range(4):
        rows = pl.ds(2 * frame, 2)
        above, below = arrived(flags, first[rows].reshape(2 * WIDTH, CHANS), second[rows].reshape(2 * WIDTH, CHANS))
        fields.append(jnp.concatenate([above, upd[frame].reshape(OWN, CHANS), below]))
    new = conv_rows(fields, side_by_side(w_res), 5).reshape(4, 5, WIDTH, CHANS)
    new = (base[...].astype(F32) + new).astype(BF16)
    out[:, 1:4] = new[:, 1:4]
    out[:, 0] = new[:, 0] * flags[4:5].astype(BF16)
    out[:, 4] = new[:, 4] * flags[5:6].astype(BF16)


def last_kernel(flags, state, upd, first, second, w_res, out):
    fields = []
    for frame in range(2):
        above, below = arrived(flags, first[frame, 0], second[frame, 0])
        fields.append(jnp.concatenate([above, upd[frame].reshape(OWN, CHANS), below]))
    new = conv_rows(fields, side_by_side(w_res), ROWS).reshape(2, ROWS, WIDTH, CHANS)
    out[...] = (state[:2, 1:4].astype(F32) + new).astype(BF16)


VM = pl.BlockSpec(memory_space=pltpu.VMEM)


def call(kernel, outs, scratch, flops, *args):
    size = sum(a.size * a.dtype.itemsize for a in args)
    return pl.pallas_call(
        kernel,
        out_shape=outs,
        in_specs=[VM] * len(args),
        out_specs=[VM] * len(outs),
        scratch_shapes=scratch,
        compiler_params=pltpu.CompilerParams(vmem_limit_bytes=14 * 2**20),
        cost_estimate=pl.CostEstimate(flops=flops, bytes_accessed=size, transcendentals=0),
    )(*args)


def slot_table(pairs, index):
    chip, core = index >> 1, index & 1
    sources, targets, owners = (pairs[:, k] for k in range(3))

    def place(frame):
        dev = (frame >> 1) - 2 * chip
        other = jnp.where((dev >= 1) != (core == 1), 4, 0)
        return other + jnp.where((dev < 0) | (dev > 1), 2, 0) + (frame & 1)

    mine = (owners >> 1) == chip
    order = jnp.arange(pairs.shape[0], dtype=jnp.int32)
    ranks = jnp.sum(jnp.where((order[None, :] < order[:, None]) & mine[None, :], 1, 0), axis=1)
    codes = place(sources) * SLOTS + place(targets)
    levels = 2 * jnp.arange(SLOTS, dtype=jnp.int32) + core
    picked = jnp.where((ranks[None, :] == levels[:, None]) & mine[None, :], codes[None, :] + 1, 0)
    picked = jnp.sum(picked, axis=1) - 1
    return picked[None]


def row_flags(row):
    line = lax.broadcasted_iota(jnp.int32, (8, CHANS), 0)
    odd, up, down = row % 2 == 1, row > 0, row < 3
    flags = ((line == 0) & (up & odd)) | ((line == 1) & (up & ~odd)) | ((line == 2) & (down & ~odd))
    flags = flags | ((line == 3) & (down & odd)) | ((line == 4) & up) | ((line == 5) & down)
    return flags.astype(F32)


def local(fmap, context, pairs, w_corr, w_zr, w_q, w_msg, w_res):
    index, row = lax.axis_index("frames"), lax.axis_index("rows")
    n_frames, n_rows = lax.axis_size("frames"), lax.axis_size("rows")
    even_swap = [(i, i ^ 1) for i in range(n_rows)]
    odd_swap = [(i, n_rows - 1 - i) for i in range(n_rows)]
    odd = row % 2 == 1
    across = [(i, (i + 2) % 4) for i in range(n_rows)]
    core_swap = [(i, i ^ 1) for i in range(n_frames)]
    partner = {i: i + 1 if i % 2 else i - 1 for i in range(1, n_frames - 1)}
    chip_swap = [
        (i * n_rows + j, partner[i] * n_rows + j if i in partner else i * n_rows + (j ^ 1))
        for i in range(n_frames)
        for j in range(n_rows)
    ]

    def rows_swaps(to_above, to_below):
        first = lax.ppermute(jnp.where(odd, to_above, to_below), "rows", even_swap)
        second = lax.ppermute(jnp.where(odd, to_below, to_above), "rows", odd_swap)
        return first, second

    def swap_core(x):
        return lax.ppermute(x, "frames", core_swap)

    def swap_chip(x):
        return lax.ppermute(x, ("frames", "rows"), chip_swap)

    with jax.named_scope("feature_rows"):
        center = jnp.concatenate([fmap, context], axis=1)
        near_center = swap_chip(center)
        far = lax.ppermute(jnp.where(row < 2, fmap[:, 2:], fmap[:, :1]), "rows", across)
        first, second = rows_swaps(
            jnp.concatenate([fmap, context[:, :1]], axis=1), jnp.concatenate([fmap, context[:, 2:]], axis=1)
        )
        none = jnp.zeros_like(far)
        blank = jnp.zeros_like(first)
        from_above = jnp.where(row > 0, jnp.where(odd, first, second), blank)
        from_below = jnp.where(row < n_rows - 1, jnp.where(odd, second, first), blank)
        halo = jnp.concatenate(
            [
                jnp.where(row < 2, none, far),
                from_above[:, :3],
                from_below[:, :3],
                jnp.where(row < 2, far, none),
                from_above[:, 3:],
                from_below[:, 3:],
            ],
            axis=1,
        )
    halo, pairs, w_corr = lax.optimization_barrier((halo, pairs, w_corr))
    idx, flags = slot_table(pairs, index), row_flags(row)
    tables = call(
        tables_kernel,
        [
            jax.ShapeDtypeStruct((WIDTH, WIDTH), BF16),
            jax.ShapeDtypeStruct((CHANS, CHANS), BF16),
            jax.ShapeDtypeStruct((WIDTH, CHANS), F32),
        ],
        [],
        2_000_000,
        w_corr,
    )
    with jax.named_scope("feature_window"):
        near_halo = swap_chip(halo)
        halo_other = swap_core(halo)
        center_other = swap_core(jnp.concatenate([center, near_center]))
        near_halo_other = swap_core(near_halo)

    with jax.named_scope("first_iteration"):
        sums = [jax.ShapeDtypeStruct((4, OWN, CHANS), BF16)] * 2
        edge_rows = [jax.ShapeDtypeStruct((SLOTS, WIDTH, CHANS), BF16)] * 2
        part, part_other, hid, hid_first, hid_last, motion, base = call(
            first_kernel,
            [
                *sums,
                jax.ShapeDtypeStruct((SLOTS, OWN, CHANS), F32),
                *edge_rows,
                jax.ShapeDtypeStruct((SLOTS, WIDE, CHANS), BF16),
                jax.ShapeDtypeStruct((4, 5, WIDTH, CHANS), BF16),
            ],
            [
                pltpu.VMEM((GROUP, 5, WIDTH, CHANS), BF16),
                pltpu.VMEM((GROUP, 11, WIDTH, CHANS), BF16),
                pltpu.VMEM((GROUP, 5, WIDTH, CHANS), BF16),
                pltpu.VMEM((SLOTS, OWN, CHANS), F32),
                pltpu.SMEM((SLOTS,), jnp.int32),
            ],
            2_000_000_000,
            idx, center, near_center, center_other, halo, near_halo, halo_other, near_halo_other, *tables, w_zr, w_q, w_msg,
        )

    with jax.named_scope("first_sums"):
        mine = part.astype(F32) + swap_core(part_other).astype(F32)
        sent = mine.astype(BF16)
        arrived = swap_chip(sent).astype(F32)
        total = mine + jnp.concatenate([arrived[2:], arrived[:2]])
        upd = jnp.maximum(total, 0.0).astype(BF16).reshape(4, ROWS, WIDTH, CHANS)
    with jax.named_scope("update_rows"):
        first, second = rows_swaps(
            jnp.concatenate([upd[:, :2].reshape(8, WIDTH, CHANS), hid_first]),
            jnp.concatenate([upd[:, 1:].reshape(8, WIDTH, CHANS), hid_last]),
        )
    with jax.named_scope("first_state"):
        [state] = call(
            state_kernel,
            [jax.ShapeDtypeStruct((4, 5, WIDTH, CHANS), BF16)],
            [],
            400_000_000,
            flags, base, upd, first, second, w_res,
        )
        state_other = swap_core(state)
    with jax.named_scope("second_iteration"):
        part, part_other = call(
            second_kernel,
            sums,
            [
                pltpu.VMEM((GROUP, 5, WIDTH, CHANS), BF16),
                pltpu.VMEM((SLOTS, OWN, CHANS), F32),
                pltpu.SMEM((SLOTS,), jnp.int32),
            ],
            1_500_000_000,
            idx, flags, state, state_other, motion, hid, first, second, w_zr, w_q, w_msg,
        )
    with jax.named_scope("second_sums"):
        mine = part.astype(F32) + swap_core(part_other).astype(F32)
        arrived = swap_chip(mine[2:].astype(BF16)).astype(F32)
        upd = jnp.maximum(mine[:2] + arrived, 0.0).astype(BF16).reshape(2, ROWS, WIDTH, CHANS)
        first, second = rows_swaps(upd[:, :1], upd[:, 2:])
    with jax.named_scope("last_state"):
        [out] = call(
            last_kernel,
            [jax.ShapeDtypeStruct((2, ROWS, WIDTH, CHANS), BF16)],
            [],
            120_000_000,
            flags, state, upd, first, second, w_res,
        )
    return out


def solution(mesh):
    placed = (
        P("frames", "rows", None, None),
        P("frames", "rows", None, None),
        P(),
        P(),
        P(),
        P(),
        P(),
        P(),
    )
    return jax.shard_map(
        local,
        mesh=mesh,
        in_specs=placed,
        out_specs=P("frames", "rows", None, None),
        check_vma=False,
    )
```
